32 devices in a mesh: section: 4 (over y, x), dp: 2 (over core), expert: 4 (over z).
Axes of the slice: x: 2, y: 2, z: 4, core: 2. Of those that a mesh axis runs over, the one named last changes fastest.
Arguments:
- tokens: bfloat16 [4, 1024, 2048], P('section', ('dp', 'expert')), may hold values from -6 to 6
- out_grad: bfloat16 [4, 1024, 2048], P('section', ('dp', 'expert')), may hold values from -6 to 6
- expert_ids: int32 [4, 1024, 2], P('section', ('dp', 'expert')), may hold values from 0 to 3, all different within a row; in each aligned block of 128 rows (0 to 127, 128 to 255, ..., all dimensions but the last counted through in order) at most 128 rows name the same one
- route_probs: float32 [4, 1024, 2], P('section', ('dp', 'expert')), may hold values from 0.1 to 1
- gate_weight: bfloat16 [4, 4, 2048, 768], P('section', 'expert', None, 'dp'), may hold values from -0.125 to 0.125
- up_weight: bfloat16 [4, 4, 2048, 768], P('section', 'expert', None, 'dp'), may hold values from -0.125 to 0.125
- down_weight: bfloat16 [4, 4, 768, 2048], P('section', 'expert', 'dp'), may hold values from -0.21875 to 0.21875
Outputs:
- grad_in: bfloat16 [4, 1024, 2048], P('section', ('dp', 'expert'))
- prob_grad: float32 [4, 1024, 2], P('section', ('dp', 'expert'))
- gate_weight_grad: bfloat16 [4, 4, 2048, 768], P('section', 'expert', None, 'dp')
- up_weight_grad: bfloat16 [4, 4, 2048, 768], P('section', 'expert', None, 'dp')
- down_weight_grad: bfloat16 [4, 4, 768, 2048], P('section', 'expert', 'dp')
The draws below stay inside these ranges and needn't reach their ends.
Inputs may be any that keep to these rules, and one draw needn't show every extreme that they name: `expert_ids`: each token names 2 different experts; among the 128 tokens of one device (aligned blocks of 128 tokens of a section) no expert is named more than 128 times, a bound that some block reaches.
All inputs are finite; a program needn't handle non-finite values.
Results may differ from the reference program's by a relative error of at most 0.023.
Values may be sent and summed in bfloat16 or wider, within the bound.
No kernel may reach another device: no remote copies, remote signals or barrier semaphores. Data moves between devices by JAX's collectives and lax.ppermute only.
A program may use at most 128 MiB of HBM per device.

```python
import math
import jax
import jax.numpy as jnp
import numpy as np
from jax import lax

D = 2048
FF = 768
TOP = 2
T_DEV = 128
SECTIONS = 4
EXPERTS = 4
TOKENS = 1024
CAP = 128
N_DP = 2


def block_levels(key, dims, pieces, smallest, top_value):
    factor_of = 1.0
    for position, parts in pieces:
        draws = jax.random.uniform(jax.random.fold_in(jax.random.fold_in(key, 6), position), (parts,), jnp.float32, smallest / len(pieces), top_value / len(pieces))
        factor_of = factor_of * jnp.repeat(jnp.exp(draws), dims[position] // parts).reshape((-1,) + (1,) * (len(dims) - 1 - position))
    return factor_of


def deal_out(own_key, own, number, rows, number_of, top, reach, skew):
    order = jax.random.permutation(own_key, number_of)
    packed, common = portions_of(number_of, rows * top, reach, skew, True), portions_of(number_of, rows * top, reach, skew, False)
    places = jnp.arange(number_of)

    def named(lengths, offset_by):
        used = int((lengths > 0).sum())
        fixed = max(1, used // 4)
        shifted = fixed + (places - fixed + offset_by * (used - fixed)) % max(1, number_of - fixed)
        return jnp.zeros((number_of,), jnp.int32).at[order[jnp.where(places < fixed, places, shifted)]].set(jnp.asarray(lengths, jnp.int32))

    lengths = jnp.where(number % 4 == 0, named(packed, number // 4), named(common, number - number // 4 - 1))
    mixed = jax.random.permutation(jax.random.fold_in(own, 3), number_of)
    source_of, receiver = mixed[0:number_of // 2 * 2:2], mixed[1:number_of // 2 * 2:2]
    room = jnp.minimum(lengths[source_of] - 1, reach - lengths[receiver]) // 2
    room = jnp.where((source_of == order[0]) | (receiver == order[0]) | (lengths[receiver] == 0), 0, jnp.maximum(room, 0))
    shifted = jax.random.randint(jax.random.fold_in(own, 4), (number_of // 2,), 0, 1 << 20) % (room + 1)
    lengths = lengths.at[source_of].add(-shifted).at[receiver].add(shifted)
    labels = jnp.searchsorted(jnp.cumsum(lengths), jnp.arange(rows * top), side="right").astype(jnp.int32)
    grid = labels.reshape(top, rows).T
    grid = grid[jax.random.permutation(jax.random.fold_in(own, 1), rows)]
    offset_by = jax.random.randint(jax.random.fold_in(own, 2), (rows, 1), 0, top)
    return jnp.take_along_axis(grid, (jnp.arange(top)[None, :] + offset_by) % top, axis=1)


def portions_of(amount, total, limit, lean, full):
    weights = [(1 << 20) // math.isqrt(standing ** lean) + 1 for standing in range(1, amount + 1)]
    largest = limit if full else min(limit, max(-(-total // amount), total * weights[0] // sum(weights)))
    least = 1 if total - largest >= amount - 1 else 0
    holding, rest = [largest] + [least] * (amount - 1), total - largest - least * (amount - 1)
    while rest > 0:
        movable = [i for i in range(1, amount) if holding[i] < largest] or [i for i in range(1, amount) if holding[i] < limit]
        mass, remaining = sum([weights[i] for i in movable]), rest
        for i in movable:
            extra = min(limit - holding[i], max(1, remaining * weights[i] // mass), rest)
            holding[i] = holding[i] + extra
            rest = rest - extra
    return np.array(holding)


def scatter_about(rng, extent, deviation, bound, cuts=(), kind=jnp.bfloat16):
    result = jax.random.normal(rng, extent, jnp.float32) * deviation
    if len(cuts) > 0:
        result = block_levels(rng, extent, cuts, -0.22, 0.18) * result
    return jnp.clip(result, min=-bound, max=bound).astype(kind)


def setup_inputs(seed: int = 0) -> dict:
    arg_keys = jax.random.split(jax.random.key(seed), 8)
    tokens = scatter_about(arg_keys[0], (SECTIONS, TOKENS, D), 1.0, 6.0, ((0, 4), (1, 8)))
    out_grad = scatter_about(arg_keys[1], (SECTIONS, TOKENS, D), 1.0, 6.0, ((0, 4), (1, 8)))
    expert_ids_keys = jax.random.split(jax.random.fold_in(arg_keys[2], 1), SECTIONS * TOKENS // T_DEV)
    expert_ids_turns = jax.random.permutation(jax.random.fold_in(arg_keys[2], 3), SECTIONS * TOKENS // T_DEV)
    expert_ids = jax.vmap(lambda own, number: deal_out(jax.random.fold_in(arg_keys[2], 2), own, number, T_DEV, EXPERTS, TOP, CAP, 2))(expert_ids_keys, expert_ids_turns).reshape((SECTIONS, TOKENS, TOP))
    route_probs = jnp.clip(0.1 + 0.9 * jax.random.uniform(arg_keys[3], (SECTIONS, TOKENS, TOP), jnp.float32) ** block_levels(arg_keys[3], (SECTIONS, TOKENS, TOP), ((0, 4), (1, 8)), -0.2, 0.2), 0.1, 1.0)
    gate_weight = scatter_about(arg_keys[4], (SECTIONS, EXPERTS, D, FF), D ** -0.5, 0.125, ((0, 4), (1, 4), (3, 2)))
    up_weight = scatter_about(arg_keys[5], (SECTIONS, EXPERTS, D, FF), D ** -0.5, 0.125, ((0, 4), (1, 4), (3, 2)))
    down_weight = scatter_about(arg_keys[6], (SECTIONS, EXPERTS, FF, D), FF ** -0.5, 0.21875, ((0, 4), (1, 4), (2, 2)))
    return dict(tokens=tokens, out_grad=out_grad, expert_ids=expert_ids, route_probs=route_probs, gate_weight=gate_weight, up_weight=up_weight, down_weight=down_weight)


def expert_grads(rows_in, grads_in, weights_in, gate_part, up_part, down_part):
    gate_pre = jnp.dot(rows_in, gate_part, preferred_element_type=jnp.float32)
    up_pre = jnp.dot(rows_in, up_part, preferred_element_type=jnp.float32)
    sigmoid_gate = jax.nn.sigmoid(gate_pre)
    activated = gate_pre * sigmoid_gate * up_pre
    scaled_act = (weights_in[:, None] * activated).astype(jnp.bfloat16)
    hidden_grad = jnp.dot(grads_in, down_part.T, preferred_element_type=jnp.float32)
    prob_part = jnp.sum(activated * hidden_grad, axis=1)
    hidden_scaled = weights_in[:, None] * hidden_grad
    gate_grad = (hidden_scaled * up_pre * sigmoid_gate * (1.0 + gate_pre * (1.0 - sigmoid_gate))).astype(jnp.bfloat16)
    up_grad = (hidden_scaled * gate_pre * sigmoid_gate).astype(jnp.bfloat16)
    route_dx = jnp.dot(gate_grad, gate_part.T, preferred_element_type=jnp.float32) + jnp.dot(up_grad, up_part.T, preferred_element_type=jnp.float32)
    grad_gate = jnp.dot(rows_in.T, gate_grad, preferred_element_type=jnp.float32)
    grad_up = jnp.dot(rows_in.T, up_grad, preferred_element_type=jnp.float32)
    grad_down = jnp.dot(scaled_act.T, grads_in, preferred_element_type=jnp.float32)
    return route_dx, prob_part, grad_gate, grad_up, grad_down


def reference(tokens, out_grad, expert_ids, route_probs, gate_weight, up_weight, down_weight):
    row_total = N_DP * EXPERTS * CAP
    token_grads, prob_grads, gate_list, up_list, down_list = [], [], [], [], []
    for section in range(SECTIONS):
        route_ids = expert_ids[section].reshape(-1)
        probs_flat = route_probs[section].reshape(-1)
        section_tokens = tokens[section]
        section_grads = out_grad[section]

        def one_expert(expert):
            hit = route_ids == expert
            picked = jnp.nonzero(hit, size=row_total, fill_value=0)[0].astype(jnp.int32)
            is_live = jnp.arange(row_total, dtype=jnp.int32) < jnp.sum(hit.astype(jnp.int32))
            token_index = picked // TOP
            zero_value = jnp.zeros((), jnp.bfloat16)
            rows_in = jnp.where(is_live[:, None], section_tokens[token_index], zero_value)
            grads_in = jnp.where(is_live[:, None], section_grads[token_index], zero_value)
            weights_in = jnp.where(is_live, probs_flat[picked], jnp.zeros((), jnp.float32))
            route_dx, prob_part, grad_gate, grad_up, grad_down = expert_grads(
                rows_in, grads_in, weights_in, gate_weight[section, expert], up_weight[section, expert], down_weight[section, expert])
            return (route_dx.astype(jnp.bfloat16), prob_part, grad_gate.astype(jnp.bfloat16),
                    grad_up.astype(jnp.bfloat16), grad_down.astype(jnp.bfloat16), picked, is_live)

        route_dx, prob_part, grad_gate, grad_up, grad_down, picked, is_live = lax.map(
            one_expert, jnp.arange(EXPERTS, dtype=jnp.int32))
        live_flat = is_live.reshape(-1)
        picked_flat = picked.reshape(-1)
        dx_flat = jnp.where(live_flat[:, None], route_dx.reshape(-1, D).astype(jnp.float32), jnp.zeros((), jnp.float32))
        summed = jnp.zeros((TOKENS * TOP, D), jnp.float32).at[picked_flat].add(dx_flat)
        token_grads.append(summed.reshape(TOKENS, TOP, D).sum(axis=1).astype(jnp.bfloat16))
        prob_flat = jnp.where(live_flat, prob_part.reshape(-1), jnp.zeros((), jnp.float32))
        prob_grads.append(jnp.zeros((TOKENS * TOP,), jnp.float32).at[picked_flat].add(prob_flat).reshape(TOKENS, TOP))
        gate_list.append(grad_gate)
        up_list.append(grad_up)
        down_list.append(grad_down)
    token_stack = jnp.stack(token_grads)
    grad_in = jnp.roll(token_stack, -1, axis=0)
    return grad_in, jnp.stack(prob_grads), jnp.stack(gate_list), jnp.stack(up_list), jnp.stack(down_list)
```

```python
import jax
import jax.numpy as jnp
from jax import lax
from jax.sharding import PartitionSpec as P


def from_behind(shard, axis, by):
    length = lax.axis_size(axis)
    return lax.ppermute(shard, axis, [(i, (i + by) % length) for i in range(length)])


def expert_grads(rows_in, grads_in, weights_in, gate_part, up_part, down_part):
    contract_last = (((1,), (1,)), ((), ()))
    contract_first = (((0,), (0,)), ((), ()))
    gate_pre = jnp.dot(rows_in, gate_part, preferred_element_type=jnp.float32)
    up_pre = jnp.dot(rows_in, up_part, preferred_element_type=jnp.float32)
    sigmoid_gate = jax.nn.sigmoid(gate_pre)
    activated = gate_pre * sigmoid_gate * up_pre
    scaled_act = (weights_in[:, None] * activated).astype(jnp.bfloat16)
    hidden_grad = lax.dot_general(
        grads_in, down_part, contract_last, preferred_element_type=jnp.float32
    )
    prob_part = jnp.sum(activated * hidden_grad, axis=1)
    hidden_scaled = weights_in[:, None] * hidden_grad
    gate_grad = (
        hidden_scaled * up_pre * sigmoid_gate * (1.0 + gate_pre * (1.0 - sigmoid_gate))
    ).astype(jnp.bfloat16)
    up_grad = (hidden_scaled * gate_pre * sigmoid_gate).astype(jnp.bfloat16)
    route_dx = lax.dot_general(
        gate_grad, gate_part, contract_last, preferred_element_type=jnp.float32
    ) + lax.dot_general(up_grad, up_part, contract_last, preferred_element_type=jnp.float32)
    grad_gate = lax.dot_general(
        rows_in, gate_grad, contract_first, preferred_element_type=jnp.float32
    )
    grad_up = lax.dot_general(rows_in, up_grad, contract_first, preferred_element_type=jnp.float32)
    grad_down = lax.dot_general(
        scaled_act, grads_in, contract_first, preferred_element_type=jnp.float32
    )
    return (route_dx, prob_part, grad_gate, grad_up, grad_down)


def exchange_plan(tokens, out_grad, expert_ids, route_probs, gate_weight, up_weight, down_weight):
    local_tokens = tokens[0]
    local_grads = out_grad[0]
    tok_count, row_width = local_tokens.shape
    top_count = expert_ids.shape[2]
    groups = lax.axis_size("expert")
    capacity = 2 * tok_count * top_count // groups
    slots_all = groups * capacity
    route_ids = expert_ids[0].reshape(-1)
    hit_table = (route_ids[:, None] == jnp.arange(groups, dtype=jnp.int32)[None, :]).astype(
        jnp.int32
    )
    before = jnp.cumsum(hit_table, axis=0) - hit_table
    slot_rank = jnp.sum(before * hit_table, axis=1)
    slot_of = route_ids * capacity + slot_rank
    placed = slot_of[None, :] == jnp.arange(slots_all, dtype=jnp.int32)[:, None]
    per_token = jnp.any(placed.reshape(slots_all, tok_count, top_count), axis=2).astype(
        jnp.bfloat16
    )
    send_rows = jnp.dot(per_token, local_tokens, preferred_element_type=jnp.float32).astype(
        jnp.bfloat16
    )
    send_grads = jnp.dot(per_token, local_grads, preferred_element_type=jnp.float32).astype(
        jnp.bfloat16
    )
    probs_flat = route_probs[0].reshape(-1)
    send_probs = jnp.sum(jnp.where(placed, probs_flat[None, :], 0.0), axis=1)
    recv_rows, recv_grads, recv_probs = (
        lax.all_to_all(
            send_rows.reshape(groups, capacity, row_width),
            "expert",
            split_axis=0,
            concat_axis=0,
            tiled=True,
        ),
        lax.all_to_all(
            send_grads.reshape(groups, capacity, row_width),
            "expert",
            split_axis=0,
            concat_axis=0,
            tiled=True,
        ),
        lax.all_to_all(
            send_probs.reshape(groups, capacity).astype(jnp.bfloat16),
            "expert",
            split_axis=0,
            concat_axis=0,
            tiled=True,
        ).astype(jnp.float32),
    )
    recv_rows = recv_rows.reshape(slots_all, row_width)
    recv_grads = recv_grads.reshape(slots_all, row_width)
    recv_probs = recv_probs.reshape(slots_all)
    gate_part = gate_weight[0, 0]
    up_part = up_weight[0, 0]
    down_part = down_weight[0, 0]
    gate_full, up_full, down_full = (
        lax.all_gather(gate_part, "dp", axis=1, tiled=True),
        lax.all_gather(up_part, "dp", axis=1, tiled=True),
        lax.all_gather(down_part, "dp", axis=0, tiled=True),
    )
    route_dx, prob_part, grad_gate, grad_up, grad_down = expert_grads(
        recv_rows, recv_grads, recv_probs, gate_full, up_full, down_full
    )
    grad_gate, grad_up, grad_down = (
        lax.psum_scatter(
            grad_gate.astype(jnp.bfloat16), "dp", scatter_dimension=1, tiled=True
        ).astype(jnp.float32),
        lax.psum_scatter(
            grad_up.astype(jnp.bfloat16), "dp", scatter_dimension=1, tiled=True
        ).astype(jnp.float32),
        lax.psum_scatter(
            grad_down.astype(jnp.bfloat16), "dp", scatter_dimension=0, tiled=True
        ).astype(jnp.float32),
    )
    back_rows, back_probs = (
        lax.all_to_all(
            route_dx.astype(jnp.bfloat16).reshape(groups, capacity, row_width),
            "expert",
            split_axis=0,
            concat_axis=0,
            tiled=True,
        ),
        lax.all_to_all(
            prob_part.reshape(groups, capacity).astype(jnp.bfloat16),
            "expert",
            split_axis=0,
            concat_axis=0,
            tiled=True,
        ).astype(jnp.float32),
    )
    token_grad = lax.dot_general(
        per_token,
        back_rows.reshape(slots_all, row_width),
        (((0,), (0,)), ((), ())),
        preferred_element_type=jnp.float32,
    ).astype(jnp.bfloat16)
    route_grad = jnp.sum(jnp.where(placed, back_probs.reshape(slots_all)[:, None], 0.0), axis=0)
    route_grad = route_grad.reshape(tok_count, top_count)
    upstream = from_behind(token_grad, "section", -1)
    return (
        upstream[None],
        route_grad[None],
        grad_gate.astype(jnp.bfloat16)[None, None],
        grad_up.astype(jnp.bfloat16)[None, None],
        grad_down.astype(jnp.bfloat16)[None, None],
    )


INWARD = [(0, 1), (3, 2)]
OUTWARD = [(1, 0), (2, 3)]
MIDDLE = [(1, 2), (2, 1)]
PAIRS = INWARD + OUTWARD
SWAP = [(0, 1), (1, 0)]


def line_plan(tokens, out_grad, expert_ids, route_probs, gate_weight, up_weight, down_weight):
    f32, bf16 = jnp.float32, jnp.bfloat16
    place = lax.axis_index("expert")
    inner = (place == 1) | (place == 2)
    tok, grd = tokens[0], out_grad[0]
    ids, probs = expert_ids[0], route_probs[0]
    half = gate_weight.shape[3]

    def over(x, pairs):
        return lax.ppermute(x, "expert", pairs)

    def pick(a, b):
        return jnp.where(inner, a, b)

    def mm(a, b, dims):
        return lax.dot_general(a, b, (dims, ((), ())), preferred_element_type=f32)

    def column(k):
        return jnp.sum(jnp.where(ids == (place ^ k), probs, 0.0), axis=1)

    def flip(x, k):
        return over(x, [(i, i ^ k) for i in range(4)])

    own_w = jnp.concatenate([gate_weight[0, 0], up_weight[0, 0]], axis=1)
    own_d = down_weight[0, 0]
    t_near = over(tok, PAIRS)
    t_mid_in = over(tok, MIDDLE)
    g_in = over(grd, INWARD)
    sib_w = lax.ppermute(own_w, "dp", SWAP)
    sib_d = lax.ppermute(own_d, "dp", SWAP)
    p_own = column(0)
    p1, p2, p3 = (flip(column(k).reshape(1, -1), k).reshape(-1) for k in (1, 2, 3))
    p_mid, p_far = pick(p3, p2), pick(p2, p3)

    t_mid_out = over(t_mid_in, OUTWARD)
    t_far_in = over(t_near, MIDDLE)
    t_far_out = over(t_far_in, OUTWARD)
    g_far_in = over(g_in, MIDDLE)
    g_far_out = over(g_far_in, OUTWARD)
    g_mid_in = over(grd, MIDDLE)
    g_mid_out = over(g_mid_in, OUTWARD)
    g_out = over(grd, OUTWARD)
    t_mid, t_far = pick(t_mid_in, t_mid_out), pick(t_far_in, t_far_out)
    g_far, g_mid, g_near = pick(g_far_in, g_far_out), pick(g_mid_in, g_mid_out), g_in + g_out

    def ahead(rows, p):
        out = []
        for w in (own_w, sib_w):
            both = mm(rows, w, ((1,), (0,)))
            gate, up = both[:, :half], both[:, half:]
            sig = jax.nn.sigmoid(gate)
            silu = gate * sig
            act = silu * up
            scaled = (p[:, None] * act).astype(bf16)
            by_gate = p[:, None] * up * sig * (1.0 + gate * (1.0 - sig))
            by_up = p[:, None] * silu
            out.append((act, scaled, by_gate, by_up))
        return out

    def behind(grads, parts):
        dots, halves, dx = 0.0, [], 0.0
        for (act, scaled, by_gate, by_up), d, w in zip(parts, (own_d, sib_d), (own_w, sib_w)):
            hidden = mm(grads, d, ((1,), (1,)))
            dots = dots + jnp.sum(act * hidden, axis=1)
            both = jnp.concatenate([hidden * by_gate, hidden * by_up], axis=1).astype(bf16)
            dx = dx + mm(both, w, ((1,), (1,)))
            halves.append(both)
        return dx.astype(bf16), dots, halves

    a_own, a_near = ahead(tok, p_own), ahead(t_near, p1)
    a_mid, a_far = ahead(t_mid, p_mid), ahead(t_far, p_far)
    dx_own, dot_own, h_own = behind(grd, a_own)
    dx_far, dot_far, h_far = behind(g_far, a_far)
    r5 = over(dx_far, INWARD)
    dx_mid, dot_mid, h_mid = behind(g_mid, a_mid)
    r4 = over(dx_mid, INWARD)
    r3 = over(dx_far + r5, MIDDLE)
    r2 = over(dx_mid + r4, MIDDLE)
    dx_near, dot_near, h_near = behind(g_near, a_near)
    r1 = over(dx_near + r3, PAIRS)

    def section_hop(x):
        n = lax.axis_size("section")
        return lax.ppermute(x, "section", [(i, (i - 1) % n) for i in range(n)])

    token_grad = (dx_own.astype(f32) + r1.astype(f32) + r2.astype(f32)).astype(bf16)
    upstream = section_hop(token_grad)

    d1 = flip(dot_near.reshape(1, -1), 1).reshape(-1)
    d2 = flip(pick(dot_far, dot_mid).reshape(1, -1), 2).reshape(-1)
    d3 = flip(pick(dot_mid, dot_far).reshape(1, -1), 3).reshape(-1)
    prob_grad = sum(
        jnp.where(ids == (place ^ k), d[:, None], 0.0) for k, d in enumerate((dot_own, d1, d2, d3))
    )

    rows = jnp.concatenate([tok, t_far, t_mid, t_near], axis=0)
    grads = jnp.concatenate([grd, g_far, g_mid, g_near], axis=0)
    slots = ((a_own, h_own), (a_far, h_far), (a_mid, h_mid), (a_near, h_near))

    def weight_grads(side):
        hs = jnp.concatenate([h[side] for _, h in slots], axis=0)
        sc = jnp.concatenate([a[side][1] for a, _ in slots], axis=0)
        return mm(rows, hs, ((0,), (0,))), mm(sc, grads, ((0,), (0,)))

    sib_gu, sib_dn = weight_grads(1)
    got_gu = lax.ppermute(sib_gu.astype(bf16), "dp", SWAP)
    got_dn = lax.ppermute(sib_dn.astype(bf16), "dp", SWAP)
    own_gu, own_dn = weight_grads(0)
    sum_gu = (own_gu + got_gu.astype(f32)).astype(bf16)
    sum_dn = (own_dn + got_dn.astype(f32)).astype(bf16)
    return (
        upstream[None],
        prob_grad[None],
        sum_gu[:, :half][None, None],
        sum_gu[:, half:][None, None],
        sum_dn[None, None],
    )


def per_device(tokens, out_grad, expert_ids, route_probs, gate_weight, up_weight, down_weight):
    count, top = expert_ids.shape[1:]
    groups = lax.axis_size("expert")
    whole_blocks = 2 * count * top // groups >= count
    plan = line_plan if groups == 4 and lax.axis_size("dp") == 2 and whole_blocks else exchange_plan
    return plan(tokens, out_grad, expert_ids, route_probs, gate_weight, up_weight, down_weight)


def solution(mesh):
    in_specs = (
        P("section", ("dp", "expert"), None),
        P("section", ("dp", "expert"), None),
        P("section", ("dp", "expert"), None),
        P("section", ("dp", "expert"), None),
        P("section", "expert", None, "dp"),
        P("section", "expert", None, "dp"),
        P("section", "expert", "dp", None),
    )
    out_specs = (
        P("section", ("dp", "expert"), None),
        P("section", ("dp", "expert"), None),
        P("section", "expert", None, "dp"),
        P("section", "expert", None, "dp"),
        P("section", "expert", "dp", None),
    )
    return jax.shard_map(
        per_device, mesh=mesh, in_specs=in_specs, out_specs=out_specs, check_vma=False
    )
```

```python
import jax
import jax.numpy as jnp
from jax import lax
from jax.sharding import PartitionSpec as P


def from_behind(shard, axis, by):
    length = lax.axis_size(axis)
    return lax.ppermute(shard, axis, [(i, (i + by) % length) for i in range(length)])


def expert_grads(rows_in, grads_in, weights_in, gate_part, up_part, down_part):
    contract_last = (((1,), (1,)), ((), ()))
    contract_first = (((0,), (0,)), ((), ()))
    gate_pre = jnp.dot(rows_in, gate_part, preferred_element_type=jnp.float32)
    up_pre = jnp.dot(rows_in, up_part, preferred_element_type=jnp.float32)
    sigmoid_gate = jax.nn.sigmoid(gate_pre)
    activated = gate_pre * sigmoid_gate * up_pre
    scaled_act = (weights_in[:, None] * activated).astype(jnp.bfloat16)
    hidden_grad = lax.dot_general(
        grads_in, down_part, contract_last, preferred_element_type=jnp.float32
    )
    prob_part = jnp.sum(activated * hidden_grad, axis=1)
    hidden_scaled = weights_in[:, None] * hidden_grad
    gate_grad = (
        hidden_scaled * up_pre * sigmoid_gate * (1.0 + gate_pre * (1.0 - sigmoid_gate))
    ).astype(jnp.bfloat16)
    up_grad = (hidden_scaled * gate_pre * sigmoid_gate).astype(jnp.bfloat16)
    route_dx = lax.dot_general(
        gate_grad, gate_part, contract_last, preferred_element_type=jnp.float32
    ) + lax.dot_general(up_grad, up_part, contract_last, preferred_element_type=jnp.float32)
    grad_gate = lax.dot_general(
        rows_in, gate_grad, contract_first, preferred_element_type=jnp.float32
    )
    grad_up = lax.dot_general(rows_in, up_grad, contract_first, preferred_element_type=jnp.float32)
    grad_down = lax.dot_general(
        scaled_act, grads_in, contract_first, preferred_element_type=jnp.float32
    )
    return (route_dx, prob_part, grad_gate, grad_up, grad_down)


def exchange_plan(tokens, out_grad, expert_ids, route_probs, gate_weight, up_weight, down_weight):
    local_tokens = tokens[0]
    local_grads = out_grad[0]
    tok_count, row_width = local_tokens.shape
    top_count = expert_ids.shape[2]
    groups = lax.axis_size("expert")
    capacity = 2 * tok_count * top_count // groups
    slots_all = groups * capacity
    route_ids = expert_ids[0].reshape(-1)
    hit_table = (route_ids[:, None] == jnp.arange(groups, dtype=jnp.int32)[None, :]).astype(
        jnp.int32
    )
    before = jnp.cumsum(hit_table, axis=0) - hit_table
    slot_rank = jnp.sum(before * hit_table, axis=1)
    slot_of = route_ids * capacity + slot_rank
    placed = slot_of[None, :] == jnp.arange(slots_all, dtype=jnp.int32)[:, None]
    per_token = jnp.any(placed.reshape(slots_all, tok_count, top_count), axis=2).astype(
        jnp.bfloat16
    )
    send_rows = jnp.dot(per_token, local_tokens, preferred_element_type=jnp.float32).astype(
        jnp.bfloat16
    )
    send_grads = jnp.dot(per_token, local_grads, preferred_element_type=jnp.float32).astype(
        jnp.bfloat16
    )
    probs_flat = route_probs[0].reshape(-1)
    send_probs = jnp.sum(jnp.where(placed, probs_flat[None, :], 0.0), axis=1)
    recv_rows, recv_grads, recv_probs = (
        lax.all_to_all(
            send_rows.reshape(groups, capacity, row_width),
            "expert",
            split_axis=0,
            concat_axis=0,
            tiled=True,
        ),
        lax.all_to_all(
            send_grads.reshape(groups, capacity, row_width),
            "expert",
            split_axis=0,
            concat_axis=0,
            tiled=True,
        ),
        lax.all_to_all(
            send_probs.reshape(groups, capacity).astype(jnp.bfloat16),
            "expert",
            split_axis=0,
            concat_axis=0,
            tiled=True,
        ).astype(jnp.float32),
    )
    recv_rows = recv_rows.reshape(slots_all, row_width)
    recv_grads = recv_grads.reshape(slots_all, row_width)
    recv_probs = recv_probs.reshape(slots_all)
    gate_part = gate_weight[0, 0]
    up_part = up_weight[0, 0]
    down_part = down_weight[0, 0]
    gate_full, up_full, down_full = (
        lax.all_gather(gate_part, "dp", axis=1, tiled=True),
        lax.all_gather(up_part, "dp", axis=1, tiled=True),
        lax.all_gather(down_part, "dp", axis=0, tiled=True),
    )
    route_dx, prob_part, grad_gate, grad_up, grad_down = expert_grads(
        recv_rows, recv_grads, recv_probs, gate_full, up_full, down_full
    )
    grad_gate, grad_up, grad_down = (
        lax.psum_scatter(
            grad_gate.astype(jnp.bfloat16), "dp", scatter_dimension=1, tiled=True
        ).astype(jnp.float32),
        lax.psum_scatter(
            grad_up.astype(jnp.bfloat16), "dp", scatter_dimension=1, tiled=True
        ).astype(jnp.float32),
        lax.psum_scatter(
            grad_down.astype(jnp.bfloat16), "dp", scatter_dimension=0, tiled=True
        ).astype(jnp.float32),
    )
    back_rows, back_probs = (
        lax.all_to_all(
            route_dx.astype(jnp.bfloat16).reshape(groups, capacity, row_width),
            "expert",
            split_axis=0,
            concat_axis=0,
            tiled=True,
        ),
        lax.all_to_all(
            prob_part.reshape(groups, capacity).astype(jnp.bfloat16),
            "expert",
            split_axis=0,
            concat_axis=0,
            tiled=True,
        ).astype(jnp.float32),
    )
    token_grad = lax.dot_general(
        per_token,
        back_rows.reshape(slots_all, row_width),
        (((0,), (0,)), ((), ())),
        preferred_element_type=jnp.float32,
    ).astype(jnp.bfloat16)
    route_grad = jnp.sum(jnp.where(placed, back_probs.reshape(slots_all)[:, None], 0.0), axis=0)
    route_grad = route_grad.reshape(tok_count, top_count)
    upstream = from_behind(token_grad, "section", -1)
    return (
        upstream[None],
        route_grad[None],
        grad_gate.astype(jnp.bfloat16)[None, None],
        grad_up.astype(jnp.bfloat16)[None, None],
        grad_down.astype(jnp.bfloat16)[None, None],
    )


INWARD = [(0, 1), (3, 2)]
OUTWARD = [(1, 0), (2, 3)]
MIDDLE = [(1, 2), (2, 1)]
PAIRS = INWARD + OUTWARD
SWAP = [(0, 1), (1, 0)]
F32, BF16 = jnp.float32, jnp.bfloat16


def line_plan(tokens, out_grad, expert_ids, route_probs, gate_weight, up_weight, down_weight):
    place = lax.axis_index("expert")
    inner = (place == 1) | (place == 2)
    tok, grd = tokens[0], out_grad[0]
    ids, probs = expert_ids[0], route_probs[0]
    half = gate_weight.shape[3]

    def over(x, pairs, name, axis="expert"):
        with jax.named_scope(name):
            return lax.ppermute(x, axis, pairs)

    def mm(a, b, dims):
        return lax.dot_general(a, b, (dims, ((), ())), preferred_element_type=F32)

    def pick(a, b):
        return jnp.where(inner, a, b)

    def small(x, k, name):
        return over(x, [(i, i ^ k) for i in range(4)], name)

    v = dict(tok=tok, grd=grd, gate=gate_weight[0, 0], up=up_weight[0, 0], own_d=down_weight[0, 0])

    def sync(**ready):
        v.update(ready)
        v.update(lax.optimization_barrier(v))

    def ahead(rows, w):
        with jax.named_scope("ahead"):
            return mm(w, rows, ((0,), (1,)))

    def ahead_both(rows):
        return [ahead(rows, v["own_w"]), ahead(rows, v["sib_w"])]

    def behind(grads, parts, p):
        with jax.named_scope("behind"):
            dots, halves, dx = 0.0, [], 0.0
            for pre, d, w in zip(parts, (v["own_d"], v["sib_d"]), (v["own_w"], v["sib_w"])):
                gate, up = pre[:half], pre[half:]
                sig = jax.nn.sigmoid(gate)
                silu = gate * sig
                act = silu * up
                by_gate = up * sig * (1.0 + gate * (1.0 - sig))
                hidden = mm(d, grads, ((1,), (1,)))
                dots = dots + jnp.sum(act * hidden, axis=0, keepdims=True)
                scaled = p * hidden
                both = jnp.concatenate([scaled * by_gate, scaled * silu], axis=0).astype(BF16)
                dx = dx + mm(both, w, ((0,), (1,)))
                halves.append((both, (p * act).astype(BF16)))
            return dx.astype(BF16), (dots, halves)

    columns = [
        jnp.sum(jnp.where(ids == (place ^ k), probs, 0.0), axis=1).reshape(1, -1) for k in range(4)
    ]
    def tick():
        return over(v["columns"][0], SWAP, "tick", "dp")

    sync(columns=columns)
    t_near = over(v["tok"], PAIRS, "t_near")
    t_mid_in = over(v["tok"], MIDDLE, "t_mid_in")
    p_near, p_cross, p_flip = (small(v["columns"][k], k, "p") for k in (1, 2, 3))
    own_w = jnp.concatenate([v["gate"], v["up"]], axis=1)
    a_own = ahead(v["tok"], own_w)
    sync(own_w=own_w, a_own=a_own)

    sync(t_near=t_near, t_mid_in=t_mid_in, p_near=p_near, p_cross=p_cross, p_flip=p_flip, tick=tick())
    g_near = over(v["grd"], PAIRS, "g_near")
    t_mid_out = over(v["t_mid_in"], OUTWARD, "t_mid_out")
    t_far_in = over(v["t_near"], MIDDLE, "t_far_in")
    sib_g = over(v["gate"], SWAP, "sib_g", "dp")
    sib_u = over(v["up"], SWAP, "sib_u", "dp")

    sync(g_near=g_near, t_far_in=t_far_in, sib_g=sib_g, sib_u=sib_u)
    g_far_in = over(v["g_near"], MIDDLE, "g_far_in")
    t_far_out = over(v["t_far_in"], OUTWARD, "t_far_out")
    g_mid_in = over(v["grd"], MIDDLE, "g_mid_in")
    sib_d = over(v["own_d"], SWAP, "sib_d", "dp")
    sib_w = jnp.concatenate([v["sib_g"], v["sib_u"]], axis=1)
    for name in ("gate", "up", "sib_g", "sib_u"):
        del v[name]
    a_own = [v["a_own"], ahead(v["tok"], sib_w)]
    sync(a_own=a_own, sib_w=sib_w)

    sync(t_mid_out=t_mid_out, g_far_in=g_far_in, tick=tick())
    g_far_out = over(v["g_far_in"], OUTWARD, "g_far_out")
    t_cross = pick(v["t_far_in"], v["t_mid_out"])
    a_near, a_cross = ahead_both(v["t_near"]), ahead_both(t_cross)
    sync(t_cross=t_cross, a_cross=a_cross, a_near=a_near)

    sync(t_far_out=t_far_out, g_mid_in=g_mid_in, sib_d=sib_d, tick=tick())
    g_mid_out = over(v["g_mid_in"], OUTWARD, "g_mid_out")
    t_flip = pick(v["t_mid_in"], v["t_far_out"])
    a_flip = ahead_both(t_flip)
    dx_own, k_own = behind(v["grd"], v["a_own"], v["columns"][0])
    sync(t_flip=t_flip, a_flip=a_flip, dx_own=dx_own, k_own=k_own)
    sync(tick=tick())

    sync(g_far_out=g_far_out)
    g_flip = pick(v["g_mid_in"], v["g_far_out"])
    dx_flip, k_flip = behind(g_flip, v["a_flip"], v["p_flip"])
    sync(g_flip=g_flip, dx_flip=dx_flip, k_flip=k_flip)
    r5 = over(v["dx_flip"], INWARD, "r5")

    sync(g_mid_out=g_mid_out)
    g_cross = pick(v["g_far_in"], v["g_mid_out"])
    dx_cross, k_cross = behind(g_cross, v["a_cross"], v["p_cross"])
    sync(g_cross=g_cross, dx_cross=dx_cross, k_cross=k_cross)
    r4 = over(v["dx_cross"], INWARD, "r4")
    dx_near, k_near = behind(v["g_near"], v["a_near"], v["p_near"])
    sync(dx_near=dx_near, k_near=k_near)

    sync(r5=r5, tick=tick())
    back = v["dx_cross"] + v["r5"]
    sync(back=back)
    r3 = over(v["back"], MIDDLE, "r3")

    def kept(which, side):
        slots = [v["k_" + name][1][side][which] for name in ("own", "near", "cross", "flip")]
        return jnp.concatenate(slots, axis=1)

    def all_rows():
        return jnp.concatenate([v["tok"], v["t_near"], v["t_cross"], v["t_flip"]], axis=0)

    def all_grads():
        return jnp.concatenate([v["grd"], v["g_near"], v["g_cross"], v["g_flip"]], axis=0)

    with jax.named_scope("weight_grads"):
        sib_gu = mm(all_rows(), kept(0, 1), ((0,), (1,))).astype(BF16)
        sib_dn = mm(kept(1, 1), all_grads(), ((1,), (0,))).astype(BF16)
    sync(sib_gu=sib_gu, sib_dn=sib_dn)

    sync(r4=r4, tick=tick())
    back = v["dx_flip"] + v["r4"]
    sync(back=back)
    r2 = over(v["back"], MIDDLE, "r2")

    sync(r3=r3)
    back = v["dx_near"] + v["r3"]
    sync(back=back)
    r1 = over(v["back"], PAIRS, "r1")
    got_gu = over(v["sib_gu"], SWAP, "got_gu", "dp")
    got_dn = over(v["sib_dn"], SWAP, "got_dn", "dp")

    sync(got_dn=got_dn, got_gu=got_gu)
    with jax.named_scope("weight_grads"):
        own_n = mm(kept(1, 0), all_grads(), ((1,), (0,))) + v["got_dn"].astype(F32)
    sync(own_n=own_n.astype(BF16))

    sync(r2=r2, r1=r1, tick=tick())
    n = lax.axis_size("section")
    total = v["dx_own"].astype(F32) + v["r1"].astype(F32) + v["r2"].astype(F32)
    sync(total=total.astype(BF16))
    upstream = over(v["total"], [(i, (i - 1) % n) for i in range(n)], "up", "section")
    with jax.named_scope("weight_grads"):
        hs = kept(0, 0)
        own_g = mm(all_rows(), hs[:half], ((0,), (1,))) + v["got_gu"][:, :half].astype(F32)
        own_u = mm(all_rows(), hs[half:], ((0,), (1,))) + v["got_gu"][:, half:].astype(F32)
    sync(own_g=own_g.astype(BF16), own_u=own_u.astype(BF16))
    dots = [v["k_own"][0]] + [
        small(v["k_" + name][0], k, "dot") for k, name in ((1, "near"), (2, "cross"), (3, "flip"))
    ]
    prob_grad = sum(
        jnp.where(ids == (place ^ k), d.reshape(-1, 1), 0.0) for k, d in enumerate(dots)
    )
    return (
        upstream[None],
        prob_grad[None],
        v["own_g"][None, None],
        v["own_u"][None, None],
        v["own_n"][None, None],
    )


def per_device(tokens, out_grad, expert_ids, route_probs, gate_weight, up_weight, down_weight):
    count, top = expert_ids.shape[1:]
    groups = lax.axis_size("expert")
    whole_blocks = 2 * count * top // groups >= count
    plan = line_plan if groups == 4 and lax.axis_size("dp") == 2 and whole_blocks else exchange_plan
    return plan(tokens, out_grad, expert_ids, route_probs, gate_weight, up_weight, down_weight)


def solution(mesh):
    in_specs = (
        P("section", ("dp", "expert"), None),
        P("section", ("dp", "expert"), None),
        P("section", ("dp", "expert"), None),
        P("section", ("dp", "expert"), None),
        P("section", "expert", None, "dp"),
        P("section", "expert", None, "dp"),
        P("section", "expert", "dp", None),
    )
    out_specs = (
        P("section", ("dp", "expert"), None),
        P("section", ("dp", "expert"), None),
        P("section", "expert", None, "dp"),
        P("section", "expert", None, "dp"),
        P("section", "expert", "dp", None),
    )
    return jax.shard_map(
        per_device, mesh=mesh, in_specs=in_specs, out_specs=out_specs, check_vma=False
    )
```

```python
import functools

import jax
import jax.numpy as jnp
from jax import lax
from jax.experimental import pallas as pl
from jax.experimental.pallas import tpu as pltpu
from jax.sharding import PartitionSpec as P


def from_behind(shard, axis, by):
    length = lax.axis_size(axis)
    return lax.ppermute(shard, axis, [(i, (i + by) % length) for i in range(length)])


def expert_grads(rows_in, grads_in, weights_in, gate_part, up_part, down_part):
    contract_last = (((1,), (1,)), ((), ()))
    contract_first = (((0,), (0,)), ((), ()))
    gate_pre = jnp.dot(rows_in, gate_part, preferred_element_type=jnp.float32)
    up_pre = jnp.dot(rows_in, up_part, preferred_element_type=jnp.float32)
    sigmoid_gate = jax.nn.sigmoid(gate_pre)
    activated = gate_pre * sigmoid_gate * up_pre
    scaled_act = (weights_in[:, None] * activated).astype(jnp.bfloat16)
    hidden_grad = lax.dot_general(
        grads_in, down_part, contract_last, preferred_element_type=jnp.float32
    )
    prob_part = jnp.sum(activated * hidden_grad, axis=1)
    hidden_scaled = weights_in[:, None] * hidden_grad
    gate_grad = (
        hidden_scaled * up_pre * sigmoid_gate * (1.0 + gate_pre * (1.0 - sigmoid_gate))
    ).astype(jnp.bfloat16)
    up_grad = (hidden_scaled * gate_pre * sigmoid_gate).astype(jnp.bfloat16)
    route_dx = lax.dot_general(
        gate_grad, gate_part, contract_last, preferred_element_type=jnp.float32
    ) + lax.dot_general(up_grad, up_part, contract_last, preferred_element_type=jnp.float32)
    grad_gate = lax.dot_general(
        rows_in, gate_grad, contract_first, preferred_element_type=jnp.float32
    )
    grad_up = lax.dot_general(rows_in, up_grad, contract_first, preferred_element_type=jnp.float32)
    grad_down = lax.dot_general(
        scaled_act, grads_in, contract_first, preferred_element_type=jnp.float32
    )
    return (route_dx, prob_part, grad_gate, grad_up, grad_down)


def exchange_plan(tokens, out_grad, expert_ids, route_probs, gate_weight, up_weight, down_weight):
    local_tokens = tokens[0]
    local_grads = out_grad[0]
    tok_count, row_width = local_tokens.shape
    top_count = expert_ids.shape[2]
    groups = lax.axis_size("expert")
    capacity = 2 * tok_count * top_count // groups
    slots_all = groups * capacity
    route_ids = expert_ids[0].reshape(-1)
    hit_table = (route_ids[:, None] == jnp.arange(groups, dtype=jnp.int32)[None, :]).astype(
        jnp.int32
    )
    before = jnp.cumsum(hit_table, axis=0) - hit_table
    slot_rank = jnp.sum(before * hit_table, axis=1)
    slot_of = route_ids * capacity + slot_rank
    placed = slot_of[None, :] == jnp.arange(slots_all, dtype=jnp.int32)[:, None]
    per_token = jnp.any(placed.reshape(slots_all, tok_count, top_count), axis=2).astype(
        jnp.bfloat16
    )
    send_rows = jnp.dot(per_token, local_tokens, preferred_element_type=jnp.float32).astype(
        jnp.bfloat16
    )
    send_grads = jnp.dot(per_token, local_grads, preferred_element_type=jnp.float32).astype(
        jnp.bfloat16
    )
    probs_flat = route_probs[0].reshape(-1)
    send_probs = jnp.sum(jnp.where(placed, probs_flat[None, :], 0.0), axis=1)
    recv_rows, recv_grads, recv_probs = (
        lax.all_to_all(
            send_rows.reshape(groups, capacity, row_width),
            "expert",
            split_axis=0,
            concat_axis=0,
            tiled=True,
        ),
        lax.all_to_all(
            send_grads.reshape(groups, capacity, row_width),
            "expert",
            split_axis=0,
            concat_axis=0,
            tiled=True,
        ),
        lax.all_to_all(
            send_probs.reshape(groups, capacity).astype(jnp.bfloat16),
            "expert",
            split_axis=0,
            concat_axis=0,
            tiled=True,
        ).astype(jnp.float32),
    )
    recv_rows = recv_rows.reshape(slots_all, row_width)
    recv_grads = recv_grads.reshape(slots_all, row_width)
    recv_probs = recv_probs.reshape(slots_all)
    gate_part = gate_weight[0, 0]
    up_part = up_weight[0, 0]
    down_part = down_weight[0, 0]
    gate_full, up_full, down_full = (
        lax.all_gather(gate_part, "dp", axis=1, tiled=True),
        lax.all_gather(up_part, "dp", axis=1, tiled=True),
        lax.all_gather(down_part, "dp", axis=0, tiled=True),
    )
    route_dx, prob_part, grad_gate, grad_up, grad_down = expert_grads(
        recv_rows, recv_grads, recv_probs, gate_full, up_full, down_full
    )
    grad_gate, grad_up, grad_down = (
        lax.psum_scatter(
            grad_gate.astype(jnp.bfloat16), "dp", scatter_dimension=1, tiled=True
        ).astype(jnp.float32),
        lax.psum_scatter(
            grad_up.astype(jnp.bfloat16), "dp", scatter_dimension=1, tiled=True
        ).astype(jnp.float32),
        lax.psum_scatter(
            grad_down.astype(jnp.bfloat16), "dp", scatter_dimension=0, tiled=True
        ).astype(jnp.float32),
    )
    back_rows, back_probs = (
        lax.all_to_all(
            route_dx.astype(jnp.bfloat16).reshape(groups, capacity, row_width),
            "expert",
            split_axis=0,
            concat_axis=0,
            tiled=True,
        ),
        lax.all_to_all(
            prob_part.reshape(groups, capacity).astype(jnp.bfloat16),
            "expert",
            split_axis=0,
            concat_axis=0,
            tiled=True,
        ).astype(jnp.float32),
    )
    token_grad = lax.dot_general(
        per_token,
        back_rows.reshape(slots_all, row_width),
        (((0,), (0,)), ((), ())),
        preferred_element_type=jnp.float32,
    ).astype(jnp.bfloat16)
    route_grad = jnp.sum(jnp.where(placed, back_probs.reshape(slots_all)[:, None], 0.0), axis=0)
    route_grad = route_grad.reshape(tok_count, top_count)
    upstream = from_behind(token_grad, "section", -1)
    return (
        upstream[None],
        route_grad[None],
        grad_gate.astype(jnp.bfloat16)[None, None],
        grad_up.astype(jnp.bfloat16)[None, None],
        grad_down.astype(jnp.bfloat16)[None, None],
    )


INWARD = [(0, 1), (3, 2)]
OUTWARD = [(1, 0), (2, 3)]
MIDDLE = [(1, 2), (2, 1)]
PAIRS = INWARD + OUTWARD
SWAP = [(0, 1), (1, 0)]
F32, BF16 = jnp.float32, jnp.bfloat16


def gather_kernel(places, *refs):
    count = len(places)
    sources, outs, sems = refs[:count], refs[count:-1], refs[-1]
    copies = []
    for i, (source, (out, rows, cols)) in enumerate(zip(sources, places)):
        target = outs[out].at[pl.ds(rows, source.shape[0]), pl.ds(cols, source.shape[1])]
        copies.append(pltpu.make_async_copy(source, target, sems.at[i]))
    for copy in copies:
        copy.start()
    for copy in copies:
        copy.wait()


def gather(name, shapes, *pieces):
    anywhere = pl.BlockSpec(memory_space=pl.ANY)
    return pl.pallas_call(
        functools.partial(gather_kernel, [piece[1:] for piece in pieces]),
        out_shape=[jax.ShapeDtypeStruct(dims, pieces[0][0].dtype) for dims in shapes],
        in_specs=[anywhere] * len(pieces),
        out_specs=[pl.BlockSpec(memory_space=pltpu.VMEM)] * len(shapes),
        scratch_shapes=[pltpu.SemaphoreType.DMA((len(pieces),))],
        compiler_params=pltpu.CompilerParams(vmem_limit_bytes=16 << 20),
        cost_estimate=pl.CostEstimate(flops=0, bytes_accessed=1 << 20, transcendentals=0),
        name=name,
    )(*(piece[0] for piece in pieces))


def line_plan(tokens, out_grad, expert_ids, route_probs, gate_weight, up_weight, down_weight):
    place = lax.axis_index("expert")
    inner = (place == 1) | (place == 2)
    tok, grd = tokens[0], out_grad[0]
    width = tok.shape[1]
    ids, probs = expert_ids[0], route_probs[0]
    half = gate_weight.shape[3]

    def over(x, pairs, name, axis="expert"):
        with jax.named_scope(name):
            return lax.ppermute(x, axis, pairs)

    def mm(a, b, dims):
        return lax.dot_general(a, b, (dims, ((), ())), preferred_element_type=F32)

    def pick(a, b):
        return jnp.where(inner, a, b)

    def small(x, k, name):
        return over(x, [(i, i ^ k) for i in range(4)], name)

    v = dict(tok=tok, grd=grd, gate=gate_weight[0, 0], up=up_weight[0, 0], own_d=down_weight[0, 0])

    def sync(**ready):
        v.update(ready)
        v.update(lax.optimization_barrier(v))

    def drop(*names):
        for name in names:
            del v[name]

    def rows_of(x, c):
        part = x.shape[0] // 2
        return x[c * part : (c + 1) * part]

    def ahead(rows, w):
        with jax.named_scope("ahead"):
            return mm(w, rows, ((0,), (1,)))

    def ahead_both(rows):
        return [ahead(rows, v["own_w"]), ahead(rows, v["sib_w"])]

    def behind(grads, parts, p):
        with jax.named_scope("behind"):
            dots, halves, dx = 0.0, [], 0.0
            both_hidden = mm(v["all_d"], grads, ((1,), (1,)))
            for side, (pre, w) in enumerate(zip(parts, (v["own_w"], v["sib_w"]))):
                gate, up = pre[:half], pre[half:]
                sig = jax.nn.sigmoid(gate)
                silu = gate * sig
                act = silu * up
                by_gate = up * sig * (1.0 + gate * (1.0 - sig))
                hidden = both_hidden[side * half :][:half]
                dots = dots + jnp.sum(act * hidden, axis=0, keepdims=True)
                scaled = p * hidden
                both = jnp.concatenate([scaled * by_gate, scaled * silu], axis=0).astype(BF16)
                dx = dx + mm(both, w, ((0,), (1,)))
                halves.append((both, (p * act).astype(BF16)))
            return dx.astype(BF16), (dots, halves)

    columns = [
        jnp.sum(jnp.where(ids == (place ^ k), probs, 0.0), axis=1).reshape(1, -1) for k in range(4)
    ]
    sync(columns=columns)
    t_near = over(v["tok"], PAIRS, "t_near")
    t_mid_in = over(v["tok"], MIDDLE, "t_mid_in")
    p_near, p_cross, p_flip = (small(v["columns"][k], k, "p") for k in (1, 2, 3))
    own_w = jnp.concatenate([v["gate"], v["up"]], axis=1)
    a_own = ahead(v["tok"], own_w)
    sync(own_w=own_w, a_own=a_own)

    sync(t_near=t_near, t_mid_in=t_mid_in, p_near=p_near, p_cross=p_cross, p_flip=p_flip)
    g_near = over(v["grd"], PAIRS, "g_near")
    t_mid_out = over(v["t_mid_in"], OUTWARD, "t_mid_out")
    t_far_in = over(v["t_near"], MIDDLE, "t_far_in")
    sib_w = over(v["own_w"], SWAP, "sib_w", "dp")
    sib_d = over(v["own_d"], SWAP, "sib_d", "dp")

    sync(g_near=g_near, t_far_in=t_far_in, sib_w=sib_w, sib_d=sib_d)
    g_far_in = over(v["g_near"], MIDDLE, "g_far_in")
    t_far_out = over(v["t_far_in"], OUTWARD, "t_far_out")
    g_mid_in = over(v["grd"], MIDDLE, "g_mid_in")
    sib_w, all_d = gather(
        "sib_w",
        [(width, 2 * half), (2 * half, width)],
        (v["sib_w"], 0, 0, 0),
        (v["own_d"], 1, 0, 0),
        (v["sib_d"], 1, half, 0),
    )
    drop("gate", "up", "own_d", "sib_d")
    a_own = [v["a_own"], ahead(v["tok"], sib_w)]
    sync(a_own=a_own, sib_w=sib_w, all_d=all_d)

    sync(t_mid_out=t_mid_out, g_far_in=g_far_in)
    g_far_out = over(v["g_far_in"], OUTWARD, "g_far_out")
    t_cross = pick(v["t_far_in"], v["t_mid_out"])
    a_near, a_cross = ahead_both(v["t_near"]), ahead_both(t_cross)
    dx_own, k_own = behind(v["grd"], v["a_own"], v["columns"][0])
    drop("t_far_in", "t_mid_out", "a_own")
    sync(t_cross=t_cross, a_cross=a_cross, a_near=a_near, dx_own=dx_own, k_own=k_own)

    sync(t_far_out=t_far_out, g_mid_in=g_mid_in)
    g_mid_out = over(v["g_mid_in"], OUTWARD, "g_mid_out")
    t_flip = pick(v["t_mid_in"], v["t_far_out"])
    a_flip = ahead_both(t_flip)
    dx_near, k_near = behind(v["g_near"], v["a_near"], v["p_near"])
    drop("t_mid_in", "t_far_out", "a_near", "p_near")
    sync(t_flip=t_flip, a_flip=a_flip, dx_near=dx_near, k_near=k_near)

    sync(g_far_out=g_far_out)
    g_flip = pick(v["g_mid_in"], v["g_far_out"])
    dx_flip, k_flip = behind(g_flip, v["a_flip"], v["p_flip"])
    drop("g_mid_in", "g_far_out", "a_flip", "p_flip")
    sync(g_flip=g_flip, dx_flip=dx_flip, k_flip=k_flip)
    r5 = over(v["dx_flip"], INWARD, "r5")

    sync(g_mid_out=g_mid_out)
    g_cross = pick(v["g_far_in"], v["g_mid_out"])
    dx_cross, k_cross = behind(g_cross, v["a_cross"], v["p_cross"])
    drop("g_far_in", "g_mid_out", "a_cross", "p_cross")
    sync(g_cross=g_cross, dx_cross=dx_cross, k_cross=k_cross)
    r4 = over(v["dx_cross"], INWARD, "r4")
    order = ("tok", "t_near", "t_cross", "t_flip")
    rows = jnp.concatenate([v[name].T for name in order], axis=1)
    grads = jnp.concatenate([v[name] for name in ("grd", "g_near", "g_cross", "g_flip")], axis=0)
    drop(*order, "grd", "g_near", "g_cross", "g_flip")
    sync(rows=rows, grads=grads)

    sync(r5=r5)
    back = v["dx_cross"] + v["r5"]
    drop("dx_cross", "r5")
    sync(back=back)
    r3 = over(v["back"], MIDDLE, "r3")
    drop("own_w", "sib_w", "all_d", "back")

    def kept(which, side, first=0, last=None):
        slots = [v["k_" + name][1][side][which][first:last] for name in ("own", "near", "cross", "flip")]
        return jnp.concatenate(slots, axis=1)

    with jax.named_scope("weight_grads"):
        sib_gu = mm(v["rows"], kept(0, 1), ((1,), (1,))).astype(BF16)
        sib_dn = mm(kept(1, 1), v["grads"], ((1,), (0,))).astype(BF16)
    sync(sib_gu=sib_gu, sib_dn=sib_dn)

    sync(r4=r4)
    back = v["dx_flip"] + v["r4"]
    drop("dx_flip", "r4")
    sync(back=back)
    r2 = over(v["back"], MIDDLE, "r2")

    sync(r3=r3)
    back = [rows_of(v["dx_near"], c) + rows_of(v["r3"], c) for c in range(2)]
    drop("dx_near", "r3")
    sync(back=back)
    r1 = [over(x, PAIRS, "r1") for x in v["back"]]
    dots = [small(v["k_" + name][0], k, "dot") for k, name in ((2, "cross"), (3, "flip"))]
    with jax.named_scope("weight_grads"):
        own_gu = mm(v["rows"], kept(0, 0), ((1,), (1,))).astype(BF16)
        own_dn = mm(kept(1, 0), v["grads"], ((1,), (0,))).astype(BF16)
    sync(own_gu=own_gu, own_dn=own_dn)


    def section_hop(r1, c):
        n = lax.axis_size("section")
        parts = (v["dx_own"], v["r2"])
        total = sum(rows_of(x, c).astype(F32) for x in parts) + r1.astype(F32)
        sync(total=total.astype(BF16))
        return over(v["total"], [(i, (i - 1) % n) for i in range(n)], "up", "section")

    sync(r2=r2, r1a=r1[0], dots=dots)
    up_a = section_hop(v["r1a"], 0)
    sync(r1b=r1[1])
    up_b = section_hop(v["r1b"], 1)
    got_gu = over(v["sib_gu"], SWAP, "got_gu", "dp")
    got_dn = over(v["sib_dn"], SWAP, "got_dn", "dp")
    upstream = jnp.concatenate([up_a, up_b], axis=0)
    sync(got_dn=got_dn, got_gu=got_gu)
    own_n = v["own_dn"] + v["got_dn"]
    own_g = v["own_gu"][:, :half] + v["got_gu"][:, :half]
    own_u = v["own_gu"][:, half:] + v["got_gu"][:, half:]
    sync(own_g=own_g, own_u=own_u, own_n=own_n)
    dots = [v["k_own"][0], small(v["k_near"][0], 1, "dot")] + v["dots"]
    prob_grad = sum(
        jnp.where(ids == (place ^ k), d.reshape(-1, 1), 0.0) for k, d in enumerate(dots)
    )
    return (
        upstream[None],
        prob_grad[None],
        v["own_g"][None, None],
        v["own_u"][None, None],
        v["own_n"][None, None],
    )


def per_device(tokens, out_grad, expert_ids, route_probs, gate_weight, up_weight, down_weight):
    count, top = expert_ids.shape[1:]
    groups = lax.axis_size("expert")
    whole_blocks = 2 * count * top // groups >= count
    plan = line_plan if groups == 4 and lax.axis_size("dp") == 2 and whole_blocks else exchange_plan
    return plan(tokens, out_grad, expert_ids, route_probs, gate_weight, up_weight, down_weight)


def solution(mesh):
    in_specs = (
        P("section", ("dp", "expert"), None),
        P("section", ("dp", "expert"), None),
        P("section", ("dp", "expert"), None),
        P("section", ("dp", "expert"), None),
        P("section", "expert", None, "dp"),
        P("section", "expert", None, "dp"),
        P("section", "expert", "dp", None),
    )
    out_specs = (
        P("section", ("dp", "expert"), None),
        P("section", ("dp", "expert"), None),
        P("section", "expert", None, "dp"),
        P("section", "expert", None, "dp"),
        P("section", "expert", "dp", None),
    )
    return jax.shard_map(
        per_device, mesh=mesh, in_specs=in_specs, out_specs=out_specs, check_vma=False
    )
```

```python
import functools
import types

import jax
import jax.numpy as jnp
from jax import lax
from jax.experimental import pallas as pl
from jax.experimental.pallas import tpu as pltpu
from jax.sharding import PartitionSpec as P


def from_behind(shard, axis, by):
    length = lax.axis_size(axis)
    return lax.ppermute(shard, axis, [(i, (i + by) % length) for i in range(length)])


def expert_grads(rows_in, grads_in, weights_in, gate_part, up_part, down_part):
    contract_last = (((1,), (1,)), ((), ()))
    contract_first = (((0,), (0,)), ((), ()))
    gate_pre = jnp.dot(rows_in, gate_part, preferred_element_type=jnp.float32)
    up_pre = jnp.dot(rows_in, up_part, preferred_element_type=jnp.float32)
    sigmoid_gate = jax.nn.sigmoid(gate_pre)
    activated = gate_pre * sigmoid_gate * up_pre
    scaled_act = (weights_in[:, None] * activated).astype(jnp.bfloat16)
    hidden_grad = lax.dot_general(
        grads_in, down_part, contract_last, preferred_element_type=jnp.float32
    )
    prob_part = jnp.sum(activated * hidden_grad, axis=1)
    hidden_scaled = weights_in[:, None] * hidden_grad
    gate_grad = (
        hidden_scaled * up_pre * sigmoid_gate * (1.0 + gate_pre * (1.0 - sigmoid_gate))
    ).astype(jnp.bfloat16)
    up_grad = (hidden_scaled * gate_pre * sigmoid_gate).astype(jnp.bfloat16)
    route_dx = lax.dot_general(
        gate_grad, gate_part, contract_last, preferred_element_type=jnp.float32
    ) + lax.dot_general(up_grad, up_part, contract_last, preferred_element_type=jnp.float32)
    grad_gate = lax.dot_general(
        rows_in, gate_grad, contract_first, preferred_element_type=jnp.float32
    )
    grad_up = lax.dot_general(rows_in, up_grad, contract_first, preferred_element_type=jnp.float32)
    grad_down = lax.dot_general(
        scaled_act, grads_in, contract_first, preferred_element_type=jnp.float32
    )
    return (route_dx, prob_part, grad_gate, grad_up, grad_down)


def exchange_plan(tokens, out_grad, expert_ids, route_probs, gate_weight, up_weight, down_weight):
    local_tokens = tokens[0]
    local_grads = out_grad[0]
    tok_count, row_width = local_tokens.shape
    top_count = expert_ids.shape[2]
    groups = lax.axis_size("expert")
    capacity = 2 * tok_count * top_count // groups
    slots_all = groups * capacity
    route_ids = expert_ids[0].reshape(-1)
    hit_table = (route_ids[:, None] == jnp.arange(groups, dtype=jnp.int32)[None, :]).astype(
        jnp.int32
    )
    before = jnp.cumsum(hit_table, axis=0) - hit_table
    slot_rank = jnp.sum(before * hit_table, axis=1)
    slot_of = route_ids * capacity + slot_rank
    placed = slot_of[None, :] == jnp.arange(slots_all, dtype=jnp.int32)[:, None]
    per_token = jnp.any(placed.reshape(slots_all, tok_count, top_count), axis=2).astype(
        jnp.bfloat16
    )
    send_rows = jnp.dot(per_token, local_tokens, preferred_element_type=jnp.float32).astype(
        jnp.bfloat16
    )
    send_grads = jnp.dot(per_token, local_grads, preferred_element_type=jnp.float32).astype(
        jnp.bfloat16
    )
    probs_flat = route_probs[0].reshape(-1)
    send_probs = jnp.sum(jnp.where(placed, probs_flat[None, :], 0.0), axis=1)
    recv_rows, recv_grads, recv_probs = (
        lax.all_to_all(
            send_rows.reshape(groups, capacity, row_width),
            "expert",
            split_axis=0,
            concat_axis=0,
            tiled=True,
        ),
        lax.all_to_all(
            send_grads.reshape(groups, capacity, row_width),
            "expert",
            split_axis=0,
            concat_axis=0,
            tiled=True,
        ),
        lax.all_to_all(
            send_probs.reshape(groups, capacity).astype(jnp.bfloat16),
            "expert",
            split_axis=0,
            concat_axis=0,
            tiled=True,
        ).astype(jnp.float32),
    )
    recv_rows = recv_rows.reshape(slots_all, row_width)
    recv_grads = recv_grads.reshape(slots_all, row_width)
    recv_probs = recv_probs.reshape(slots_all)
    gate_part = gate_weight[0, 0]
    up_part = up_weight[0, 0]
    down_part = down_weight[0, 0]
    gate_full, up_full, down_full = (
        lax.all_gather(gate_part, "dp", axis=1, tiled=True),
        lax.all_gather(up_part, "dp", axis=1, tiled=True),
        lax.all_gather(down_part, "dp", axis=0, tiled=True),
    )
    route_dx, prob_part, grad_gate, grad_up, grad_down = expert_grads(
        recv_rows, recv_grads, recv_probs, gate_full, up_full, down_full
    )
    grad_gate, grad_up, grad_down = (
        lax.psum_scatter(
            grad_gate.astype(jnp.bfloat16), "dp", scatter_dimension=1, tiled=True
        ).astype(jnp.float32),
        lax.psum_scatter(
            grad_up.astype(jnp.bfloat16), "dp", scatter_dimension=1, tiled=True
        ).astype(jnp.float32),
        lax.psum_scatter(
            grad_down.astype(jnp.bfloat16), "dp", scatter_dimension=0, tiled=True
        ).astype(jnp.float32),
    )
    back_rows, back_probs = (
        lax.all_to_all(
            route_dx.astype(jnp.bfloat16).reshape(groups, capacity, row_width),
            "expert",
            split_axis=0,
            concat_axis=0,
            tiled=True,
        ),
        lax.all_to_all(
            prob_part.reshape(groups, capacity).astype(jnp.bfloat16),
            "expert",
            split_axis=0,
            concat_axis=0,
            tiled=True,
        ).astype(jnp.float32),
    )
    token_grad = lax.dot_general(
        per_token,
        back_rows.reshape(slots_all, row_width),
        (((0,), (0,)), ((), ())),
        preferred_element_type=jnp.float32,
    ).astype(jnp.bfloat16)
    route_grad = jnp.sum(jnp.where(placed, back_probs.reshape(slots_all)[:, None], 0.0), axis=0)
    route_grad = route_grad.reshape(tok_count, top_count)
    upstream = from_behind(token_grad, "section", -1)
    return (
        upstream[None],
        route_grad[None],
        grad_gate.astype(jnp.bfloat16)[None, None],
        grad_up.astype(jnp.bfloat16)[None, None],
        grad_down.astype(jnp.bfloat16)[None, None],
    )


INWARD = [(0, 1), (3, 2)]
OUTWARD = [(1, 0), (2, 3)]
MIDDLE = [(1, 2), (2, 1)]
PAIRS = INWARD + OUTWARD
SWAP = [(0, 1), (1, 0)]
F32, BF16 = jnp.float32, jnp.bfloat16


def gather_kernel(places, *refs):
    count = len(places)
    sources, outs, sems = refs[:count], refs[count:-1], refs[-1]
    copies = []
    for i, (source, (out, rows, cols)) in enumerate(zip(sources, places)):
        target = outs[out].at[pl.ds(rows, source.shape[0]), pl.ds(cols, source.shape[1])]
        copies.append(pltpu.make_async_copy(source, target, sems.at[i]))
    for copy in copies:
        copy.start()
    for copy in copies:
        copy.wait()


def gather(name, shapes, *pieces):
    anywhere = pl.BlockSpec(memory_space=pl.ANY)
    return pl.pallas_call(
        functools.partial(gather_kernel, [piece[1:] for piece in pieces]),
        out_shape=[pltpu.VMEM(dims, pieces[0][0].dtype) for dims in shapes],
        in_specs=[anywhere] * len(pieces),
        out_specs=[pl.BlockSpec(memory_space=pltpu.VMEM)] * len(shapes),
        scratch_shapes=[pltpu.SemaphoreType.DMA((len(pieces),))],
        compiler_params=pltpu.CompilerParams(vmem_limit_bytes=16 << 20),
        cost_estimate=pl.CostEstimate(flops=0, bytes_accessed=1 << 20, transcendentals=0),
        name=name,
    )(*(piece[0] for piece in pieces))


def line_plan(tokens, out_grad, expert_ids, route_probs, gate_weight, up_weight, down_weight):
    place = lax.axis_index("expert")
    inner = (place == 1) | (place == 2)
    tok, grd = tokens[0], out_grad[0]
    count, width = tok.shape
    ids, probs = expert_ids[0], route_probs[0]
    half = gate_weight.shape[3]

    def over(x, pairs, name, axis="expert"):
        with jax.named_scope(name):
            return lax.ppermute(x, axis, pairs)

    def mm(a, b, dims):
        return lax.dot_general(a, b, (dims, ((), ())), preferred_element_type=F32)

    def pick(a, b):
        return jnp.where(inner, a, b)

    def small(x, k, name):
        return over(x, [(i, i ^ k) for i in range(4)], name)

    v = types.SimpleNamespace(
        tok=tok, grd=grd, gate=gate_weight[0, 0], up=up_weight[0, 0], own_d=down_weight[0, 0]
    )

    def sync(**ready):
        vars(v).update(ready)
        vars(v).update(lax.optimization_barrier(vars(v)))

    def rows_of(x, c):
        part = x.shape[0] // 2
        return x[c * part : (c + 1) * part]

    def ahead(rows, w):
        with jax.named_scope("ahead"):
            return mm(w, rows, ((0,), (1,)))

    def ahead_both(rows):
        return [ahead(rows, v.own_w), ahead(rows, v.sib_w)]

    def behind(grads, parts, p):
        with jax.named_scope("behind"):
            dots, halves, dx = 0.0, [], 0.0
            both_hidden = mm(v.all_d, grads, ((1,), (1,)))
            for side, (pre, w) in enumerate(zip(parts, (v.own_w, v.sib_w))):
                gate, up = pre[:half], pre[half:]
                sig = jax.nn.sigmoid(gate)
                silu = gate * sig
                act = silu * up
                by_gate = up * sig * (1.0 + gate * (1.0 - sig))
                hidden = both_hidden[side * half :][:half]
                dots = dots + jnp.sum(act * hidden, axis=0, keepdims=True)
                scaled = p * hidden
                both = jnp.concatenate([scaled * by_gate, scaled * silu], axis=0).astype(BF16)
                dx = dx + mm(both, w, ((0,), (1,)))
                halves.append((both, (p * act).astype(BF16)))
            return dx.astype(BF16), (dots, halves)

    columns = [
        jnp.sum(jnp.where(ids == (place ^ k), probs, 0.0), axis=1).reshape(1, -1) for k in range(4)
    ]
    sync(columns=columns)
    t_near = over(v.tok, PAIRS, "t_near")
    t_mid_in = over(v.tok, MIDDLE, "t_mid_in")
    p_near, p_cross, p_flip = (small(v.columns[k], k, "p") for k in (1, 2, 3))
    (own_w,) = gather("own_w", [(width, 2 * half)], (v.gate, 0, 0, 0), (v.up, 0, 0, half))
    sync(own_w=own_w)

    sync(t_near=t_near, t_mid_in=t_mid_in, p_near=p_near, p_cross=p_cross, p_flip=p_flip)
    g_near = over(v.grd, PAIRS, "g_near")
    t_mid_out = over(v.t_mid_in, OUTWARD, "t_mid_out")
    t_far_in = over(v.t_near, MIDDLE, "t_far_in")
    sib_w = over(v.own_w, SWAP, "sib_w", "dp")
    sib_d = over(v.own_d, SWAP, "sib_d", "dp")
    t_two = jnp.concatenate([v.tok, v.t_near], axis=0)
    a_two = ahead(t_two, v.own_w)
    sync(t_two=t_two, a_two=a_two)

    sync(g_near=g_near)
    g_far_in = over(v.g_near, MIDDLE, "g_far_in")
    sync(t_far_in=t_far_in, sib_w=sib_w, sib_d=sib_d)
    t_far_out = over(v.t_far_in, OUTWARD, "t_far_out")
    sib_w, all_d = gather(
        "sib_w",
        [(width, 2 * half), (2 * half, width)],
        (v.sib_w, 0, 0, 0),
        (v.own_d, 1, 0, 0),
        (v.sib_d, 1, half, 0),
    )
    del v.gate, v.up, v.own_d, v.sib_d
    a_two = [v.a_two, ahead(v.t_two, sib_w)]
    del v.t_two
    sync(a_two=a_two, sib_w=sib_w, all_d=all_d)

    sync(t_mid_out=t_mid_out, g_far_in=g_far_in)
    g_far_out = over(v.g_far_in, OUTWARD, "g_far_out")
    g_mid_in = over(v.grd, MIDDLE, "g_mid_in")

    two = jnp.concatenate([v.grd, v.g_near], axis=0)
    dx_two, k_two = behind(two, v.a_two, jnp.concatenate([v.columns[0], v.p_near], axis=1))
    del v.p_near, v.a_two, v.columns
    sync(dx_two=dx_two, k_two=k_two)

    sync(t_far_out=t_far_out)
    t_cross, t_flip = pick(v.t_far_in, v.t_mid_out), pick(v.t_mid_in, v.t_far_out)
    del v.t_far_in, v.t_mid_out, v.t_mid_in, v.t_far_out
    a_far = ahead_both(jnp.concatenate([t_cross, t_flip], axis=0))
    sync(t_cross=t_cross, t_flip=t_flip, a_far=a_far)

    sync(g_mid_in=g_mid_in)
    g_mid_out = over(v.g_mid_in, OUTWARD, "g_mid_out")
    rows = jnp.concatenate([v.tok.T, v.t_near.T, v.t_cross.T, v.t_flip.T], axis=1)
    del v.tok, v.t_near, v.t_cross, v.t_flip
    sync(rows=rows)
    sync(g_far_out=g_far_out)
    g_flip = pick(v.g_mid_in, v.g_far_out)
    dx_flip, k_flip = behind(g_flip, [a[:, count:] for a in v.a_far], v.p_flip)
    del v.g_mid_in, v.g_far_out, v.p_flip
    sync(g_flip=g_flip, dx_flip=dx_flip, k_flip=k_flip)
    r5 = over(v.dx_flip, INWARD, "r5")

    sync(g_mid_out=g_mid_out)
    g_cross = pick(v.g_far_in, v.g_mid_out)
    dx_cross, k_cross = behind(g_cross, [a[:, :count] for a in v.a_far], v.p_cross)
    del v.g_far_in, v.g_mid_out, v.a_far, v.p_cross
    sync(g_cross=g_cross, dx_cross=dx_cross, k_cross=k_cross)
    r4 = over(v.dx_cross, INWARD, "r4")

    sync(r5=r5)
    back = v.dx_cross + v.r5
    del v.dx_cross, v.r5
    sync(back=back)
    r3 = over(v.back, MIDDLE, "r3")
    grads = jnp.concatenate([v.grd, v.g_near, v.g_cross, v.g_flip], axis=0)
    del v.grd, v.g_near, v.g_cross, v.g_flip
    sync(grads=grads)
    del v.own_w, v.sib_w, v.all_d, v.back

    def kept(which, side, first=0, last=None):
        slots = [k[1][side][which][first:last] for k in (v.k_two, v.k_cross, v.k_flip)]
        return jnp.concatenate(slots, axis=1)

    with jax.named_scope("weight_grads"):
        sib_gu = mm(v.rows, kept(0, 1), ((1,), (1,))).astype(BF16)
        sib_dn = mm(kept(1, 1), v.grads, ((1,), (0,))).astype(BF16)
    sync(sib_gu=sib_gu, sib_dn=sib_dn)

    sync(r4=r4)
    sync(r3=r3)
    back_mid = v.dx_flip + v.r4
    back = v.dx_two[count:] + v.r3
    del v.dx_flip, v.r4, v.r3
    sync(back=back, back_mid=back_mid)
    r1 = over(v.back, PAIRS, "r1")
    r2 = over(v.back_mid, MIDDLE, "r2")
    got_gu = over(v.sib_gu, SWAP, "got_gu", "dp")
    got_dn = over(v.sib_dn, SWAP, "got_dn", "dp")
    with jax.named_scope("weight_grads"):
        own_gu = mm(v.rows, kept(0, 0), ((1,), (1,))).astype(BF16)
        own_dn = mm(kept(1, 0), v.grads, ((1,), (0,))).astype(BF16)
    sync(own_gu=own_gu, own_dn=own_dn)


    sync(r1=r1)
    sync(r2=r2)
    n = lax.axis_size("section")
    total = sum(x.astype(F32) for x in (v.dx_two[:count], v.r1, v.r2))
    sync(total=total.astype(BF16))
    upstream = over(v.total, [(i, (i - 1) % n) for i in range(n)], "up", "section")
    sync(got_dn=got_dn, got_gu=got_gu)
    own_n = v.own_dn + v.got_dn
    own_g = v.own_gu[:, :half] + v.got_gu[:, :half]
    own_u = v.own_gu[:, half:] + v.got_gu[:, half:]
    sync(own_g=own_g, own_u=own_u, own_n=own_n)
    two = v.k_two[0]
    dots = (two[:, count:], v.k_cross[0], v.k_flip[0])
    dots = [two[:, :count]] + [small(d, k, "dot") for k, d in enumerate(dots, 1)]
    prob_grad = sum(
        jnp.where(ids == (place ^ k), d.reshape(-1, 1), 0.0) for k, d in enumerate(dots)
    )
    return (
        upstream[None],
        prob_grad[None],
        v.own_g[None, None],
        v.own_u[None, None],
        v.own_n[None, None],
    )


def per_device(tokens, out_grad, expert_ids, route_probs, gate_weight, up_weight, down_weight):
    count, top = expert_ids.shape[1:]
    groups = lax.axis_size("expert")
    whole_blocks = 2 * count * top // groups >= count
    plan = line_plan if groups == 4 and lax.axis_size("dp") == 2 and whole_blocks else exchange_plan
    return plan(tokens, out_grad, expert_ids, route_probs, gate_weight, up_weight, down_weight)


def solution(mesh):
    in_specs = (
        P("section", ("dp", "expert"), None),
        P("section", ("dp", "expert"), None),
        P("section", ("dp", "expert"), None),
        P("section", ("dp", "expert"), None),
        P("section", "expert", None, "dp"),
        P("section", "expert", None, "dp"),
        P("section", "expert", "dp", None),
    )
    out_specs = (
        P("section", ("dp", "expert"), None),
        P("section", ("dp", "expert"), None),
        P("section", "expert", None, "dp"),
        P("section", "expert", None, "dp"),
        P("section", "expert", "dp", None),
    )
    return jax.shard_map(
        per_device, mesh=mesh, in_specs=in_specs, out_specs=out_specs, check_vma=False
    )
```

```python
import functools
import types

import jax
import jax.numpy as jnp
from jax import lax
from jax.experimental import pallas as pl
from jax.experimental.pallas import tpu as pltpu
from jax.sharding import PartitionSpec as P


def from_behind(shard, axis, by):
    length = lax.axis_size(axis)
    return lax.ppermute(shard, axis, [(i, (i + by) % length) for i in range(length)])


def expert_grads(rows_in, grads_in, weights_in, gate_part, up_part, down_part):
    contract_last = (((1,), (1,)), ((), ()))
    contract_first = (((0,), (0,)), ((), ()))
    gate_pre = jnp.dot(rows_in, gate_part, preferred_element_type=jnp.float32)
    up_pre = jnp.dot(rows_in, up_part, preferred_element_type=jnp.float32)
    sigmoid_gate = jax.nn.sigmoid(gate_pre)
    activated = gate_pre * sigmoid_gate * up_pre
    scaled_act = (weights_in[:, None] * activated).astype(jnp.bfloat16)
    hidden_grad = lax.dot_general(
        grads_in, down_part, contract_last, preferred_element_type=jnp.float32
    )
    prob_part = jnp.sum(activated * hidden_grad, axis=1)
    hidden_scaled = weights_in[:, None] * hidden_grad
    gate_grad = (
        hidden_scaled * up_pre * sigmoid_gate * (1.0 + gate_pre * (1.0 - sigmoid_gate))
    ).astype(jnp.bfloat16)
    up_grad = (hidden_scaled * gate_pre * sigmoid_gate).astype(jnp.bfloat16)
    route_dx = lax.dot_general(
        gate_grad, gate_part, contract_last, preferred_element_type=jnp.float32
    ) + lax.dot_general(up_grad, up_part, contract_last, preferred_element_type=jnp.float32)
    grad_gate = lax.dot_general(
        rows_in, gate_grad, contract_first, preferred_element_type=jnp.float32
    )
    grad_up = lax.dot_general(rows_in, up_grad, contract_first, preferred_element_type=jnp.float32)
    grad_down = lax.dot_general(
        scaled_act, grads_in, contract_first, preferred_element_type=jnp.float32
    )
    return (route_dx, prob_part, grad_gate, grad_up, grad_down)


def exchange_plan(tokens, out_grad, expert_ids, route_probs, gate_weight, up_weight, down_weight):
    local_tokens = tokens[0]
    local_grads = out_grad[0]
    tok_count, row_width = local_tokens.shape
    top_count = expert_ids.shape[2]
    groups = lax.axis_size("expert")
    capacity = 2 * tok_count * top_count // groups
    slots_all = groups * capacity
    route_ids = expert_ids[0].reshape(-1)
    hit_table = (route_ids[:, None] == jnp.arange(groups, dtype=jnp.int32)[None, :]).astype(
        jnp.int32
    )
    before = jnp.cumsum(hit_table, axis=0) - hit_table
    slot_rank = jnp.sum(before * hit_table, axis=1)
    slot_of = route_ids * capacity + slot_rank
    placed = slot_of[None, :] == jnp.arange(slots_all, dtype=jnp.int32)[:, None]
    per_token = jnp.any(placed.reshape(slots_all, tok_count, top_count), axis=2).astype(
        jnp.bfloat16
    )
    send_rows = jnp.dot(per_token, local_tokens, preferred_element_type=jnp.float32).astype(
        jnp.bfloat16
    )
    send_grads = jnp.dot(per_token, local_grads, preferred_element_type=jnp.float32).astype(
        jnp.bfloat16
    )
    probs_flat = route_probs[0].reshape(-1)
    send_probs = jnp.sum(jnp.where(placed, probs_flat[None, :], 0.0), axis=1)
    recv_rows, recv_grads, recv_probs = (
        lax.all_to_all(
            send_rows.reshape(groups, capacity, row_width),
            "expert",
            split_axis=0,
            concat_axis=0,
            tiled=True,
        ),
        lax.all_to_all(
            send_grads.reshape(groups, capacity, row_width),
            "expert",
            split_axis=0,
            concat_axis=0,
            tiled=True,
        ),
        lax.all_to_all(
            send_probs.reshape(groups, capacity).astype(jnp.bfloat16),
            "expert",
            split_axis=0,
            concat_axis=0,
            tiled=True,
        ).astype(jnp.float32),
    )
    recv_rows = recv_rows.reshape(slots_all, row_width)
    recv_grads = recv_grads.reshape(slots_all, row_width)
    recv_probs = recv_probs.reshape(slots_all)
    gate_part = gate_weight[0, 0]
    up_part = up_weight[0, 0]
    down_part = down_weight[0, 0]
    gate_full, up_full, down_full = (
        lax.all_gather(gate_part, "dp", axis=1, tiled=True),
        lax.all_gather(up_part, "dp", axis=1, tiled=True),
        lax.all_gather(down_part, "dp", axis=0, tiled=True),
    )
    route_dx, prob_part, grad_gate, grad_up, grad_down = expert_grads(
        recv_rows, recv_grads, recv_probs, gate_full, up_full, down_full
    )
    grad_gate, grad_up, grad_down = (
        lax.psum_scatter(
            grad_gate.astype(jnp.bfloat16), "dp", scatter_dimension=1, tiled=True
        ).astype(jnp.float32),
        lax.psum_scatter(
            grad_up.astype(jnp.bfloat16), "dp", scatter_dimension=1, tiled=True
        ).astype(jnp.float32),
        lax.psum_scatter(
            grad_down.astype(jnp.bfloat16), "dp", scatter_dimension=0, tiled=True
        ).astype(jnp.float32),
    )
    back_rows, back_probs = (
        lax.all_to_all(
            route_dx.astype(jnp.bfloat16).reshape(groups, capacity, row_width),
            "expert",
            split_axis=0,
            concat_axis=0,
            tiled=True,
        ),
        lax.all_to_all(
            prob_part.reshape(groups, capacity).astype(jnp.bfloat16),
            "expert",
            split_axis=0,
            concat_axis=0,
            tiled=True,
        ).astype(jnp.float32),
    )
    token_grad = lax.dot_general(
        per_token,
        back_rows.reshape(slots_all, row_width),
        (((0,), (0,)), ((), ())),
        preferred_element_type=jnp.float32,
    ).astype(jnp.bfloat16)
    route_grad = jnp.sum(jnp.where(placed, back_probs.reshape(slots_all)[:, None], 0.0), axis=0)
    route_grad = route_grad.reshape(tok_count, top_count)
    upstream = from_behind(token_grad, "section", -1)
    return (
        upstream[None],
        route_grad[None],
        grad_gate.astype(jnp.bfloat16)[None, None],
        grad_up.astype(jnp.bfloat16)[None, None],
        grad_down.astype(jnp.bfloat16)[None, None],
    )


INWARD = [(0, 1), (3, 2)]
OUTWARD = [(1, 0), (2, 3)]
MIDDLE = [(1, 2), (2, 1)]
PAIRS = INWARD + OUTWARD
SWAP = [(0, 1), (1, 0)]
F32, BF16 = jnp.float32, jnp.bfloat16


def gather_kernel(places, *refs):
    count = len(places)
    sources, outs, sems = refs[:count], refs[count:-1], refs[-1]
    copies = []
    for i, (source, (out, rows, cols)) in enumerate(zip(sources, places)):
        target = outs[out].at[pl.ds(rows, source.shape[0]), pl.ds(cols, source.shape[1])]
        copies.append(pltpu.make_async_copy(source, target, sems.at[i]))
    for copy in copies:
        copy.start()
    for copy in copies:
        copy.wait()


def gather(name, shapes, *pieces):
    anywhere = pl.BlockSpec(memory_space=pl.ANY)
    return pl.pallas_call(
        functools.partial(gather_kernel, [piece[1:] for piece in pieces]),
        out_shape=[pltpu.VMEM(dims, pieces[0][0].dtype) for dims in shapes],
        in_specs=[anywhere] * len(pieces),
        out_specs=[pl.BlockSpec(memory_space=pltpu.VMEM)] * len(shapes),
        scratch_shapes=[pltpu.SemaphoreType.DMA((len(pieces),))],
        compiler_params=pltpu.CompilerParams(vmem_limit_bytes=16 << 20),
        cost_estimate=pl.CostEstimate(flops=0, bytes_accessed=1 << 20, transcendentals=0),
        name=name,
    )(*(piece[0] for piece in pieces))


def line_plan(tokens, out_grad, expert_ids, route_probs, gate_weight, up_weight, down_weight):
    place = lax.axis_index("expert")
    inner = (place == 1) | (place == 2)
    tok, grd = tokens[0], out_grad[0]
    count, width = tok.shape
    ids, probs = expert_ids[0], route_probs[0]
    half = gate_weight.shape[3]

    def over(x, pairs, name, axis="expert"):
        with jax.named_scope(name):
            return lax.ppermute(x, axis, pairs)

    def mm(a, b, dims):
        return lax.dot_general(a, b, (dims, ((), ())), preferred_element_type=F32)

    def pick(a, b):
        return jnp.where(inner, a, b)

    def small(x, k, name):
        return over(x, [(i, i ^ k) for i in range(4)], name)

    v = types.SimpleNamespace(
        tok=tok, grd=grd, gate=gate_weight[0, 0], up=up_weight[0, 0], own_d=down_weight[0, 0]
    )

    def sync(**ready):
        vars(v).update(ready)
        vars(v).update(lax.optimization_barrier(vars(v)))

    def rows_of(x, c):
        part = x.shape[0] // 2
        return x[c * part : (c + 1) * part]

    def ahead(rows, w):
        with jax.named_scope("ahead"):
            return mm(w, rows, ((0,), (1,)))

    def ahead_both(rows):
        return [ahead(rows, v.own_w), ahead(rows, v.sib_w)]

    def behind(grads, parts, p):
        with jax.named_scope("behind"):
            dots, halves, dx = 0.0, [], 0.0
            both_hidden = mm(v.all_d, grads, ((1,), (1,)))
            for side, (pre, w) in enumerate(zip(parts, (v.own_w, v.sib_w))):
                gate, up = pre[:half], pre[half:]
                sig = jax.nn.sigmoid(gate)
                silu = gate * sig
                act = silu * up
                by_gate = up * sig * (1.0 + gate * (1.0 - sig))
                hidden = both_hidden[side * half :][:half]
                dots = dots + jnp.sum(act * hidden, axis=0, keepdims=True)
                scaled = p * hidden
                both = jnp.concatenate([scaled * by_gate, scaled * silu], axis=0).astype(BF16)
                dx = dx + mm(both, w, ((0,), (1,)))
                halves.append((both, (p * act).astype(BF16)))
            return dx.astype(BF16), (dots, halves)

    columns = [
        jnp.sum(jnp.where(ids == (place ^ k), probs, 0.0), axis=1).reshape(1, -1) for k in range(4)
    ]
    v.columns = columns
    t_near = over(v.tok, PAIRS, "t_near")
    t_mid_in = over(v.tok, MIDDLE, "t_mid_in")
    p_near, p_cross, p_flip = (small(v.columns[k], k, "p") for k in (1, 2, 3))
    (own_w,) = gather("own_w", [(width, 2 * half)], (v.gate, 0, 0, 0), (v.up, 0, 0, half))
    sync(own_w=own_w)

    sync(t_near=t_near, t_mid_in=t_mid_in, p_near=p_near, p_cross=p_cross, p_flip=p_flip)
    g_near = over(v.grd, PAIRS, "g_near")
    t_mid_out = over(v.t_mid_in, OUTWARD, "t_mid_out")
    t_far_in = over(v.t_near, MIDDLE, "t_far_in")
    sib_w = over(v.own_w, SWAP, "sib_w", "dp")
    sib_d = over(v.own_d, SWAP, "sib_d", "dp")
    t_two = jnp.concatenate([v.tok, v.t_near], axis=0)
    a_two = ahead(t_two, v.own_w)
    sync(t_two=t_two, a_two=a_two)

    sync(g_near=g_near)
    g_far_in = over(v.g_near, MIDDLE, "g_far_in")
    sync(t_far_in=t_far_in, sib_w=sib_w, sib_d=sib_d)
    t_far_out = over(v.t_far_in, OUTWARD, "t_far_out")
    sib_w, all_d = gather(
        "sib_w",
        [(width, 2 * half), (2 * half, width)],
        (v.sib_w, 0, 0, 0),
        (v.own_d, 1, 0, 0),
        (v.sib_d, 1, half, 0),
    )
    del v.gate, v.up, v.own_d, v.sib_d
    a_two = [v.a_two, ahead(v.t_two, sib_w)]
    del v.t_two
    sync(a_two=a_two, sib_w=sib_w, all_d=all_d)

    two = jnp.concatenate([v.grd, v.g_near], axis=0)
    dx_two, k_two = behind(two, v.a_two, jnp.concatenate([v.columns[0], v.p_near], axis=1))
    del v.p_near, v.a_two, v.columns
    sync(dx_two=dx_two, k_two=k_two)
    n = lax.axis_size("section")

    def home(x, pairs, name):
        steps = [(4 * i + a, (i - 1) % n * 4 + b) for i in range(n) for a, b in pairs]
        return over(x, steps, name, ("section", "expert"))

    up_own = over(v.dx_two[:count], [(i, (i - 1) % n) for i in range(n)], "up", "section")
    up_near = home(v.dx_two[count:], INWARD, "up")

    sync(t_mid_out=t_mid_out, g_far_in=g_far_in)
    g_far_out = over(v.g_far_in, OUTWARD, "g_far_out")
    g_mid_in = over(v.grd, MIDDLE, "g_mid_in")

    sync(t_far_out=t_far_out)
    t_cross, t_flip = pick(v.t_far_in, v.t_mid_out), pick(v.t_mid_in, v.t_far_out)
    del v.t_far_in, v.t_mid_out, v.t_mid_in, v.t_far_out
    a_far = ahead_both(jnp.concatenate([t_cross, t_flip], axis=0))
    sync(t_cross=t_cross, t_flip=t_flip, a_far=a_far)

    sync(g_mid_in=g_mid_in)
    g_mid_out = over(v.g_mid_in, OUTWARD, "g_mid_out")
    rows = jnp.concatenate([v.tok.T, v.t_near.T, v.t_cross.T, v.t_flip.T], axis=1)
    del v.tok, v.t_near, v.t_cross, v.t_flip
    sync(rows=rows)
    sync(g_far_out=g_far_out)
    g_flip = pick(v.g_mid_in, v.g_far_out)
    dx_flip, k_flip = behind(g_flip, [a[:, count:] for a in v.a_far], v.p_flip)
    del v.g_mid_in, v.g_far_out, v.p_flip
    sync(g_flip=g_flip, dx_flip=dx_flip, k_flip=k_flip)
    r5 = over(v.dx_flip, INWARD, "r5")

    sync(g_mid_out=g_mid_out)
    g_cross = pick(v.g_far_in, v.g_mid_out)
    dx_cross, k_cross = behind(g_cross, [a[:, :count] for a in v.a_far], v.p_cross)
    del v.g_far_in, v.g_mid_out, v.a_far, v.p_cross
    sync(g_cross=g_cross, dx_cross=dx_cross, k_cross=k_cross)
    r4 = over(v.dx_cross, INWARD, "r4")

    sync(r5=r5, up_own=up_own, up_near=up_near)
    back = v.dx_cross + v.r5
    del v.dx_cross, v.r5
    sync(back=back)
    r3 = over(v.back, MIDDLE, "r3")
    grads = jnp.concatenate([v.grd, v.g_near, v.g_cross, v.g_flip], axis=0)
    del v.grd, v.g_near, v.g_cross, v.g_flip
    sync(grads=grads)
    del v.own_w, v.sib_w, v.all_d, v.back

    def kept(which, side, first=0, last=None):
        slots = [k[1][side][which][first:last] for k in (v.k_two, v.k_cross, v.k_flip)]
        return jnp.concatenate(slots, axis=1)

    with jax.named_scope("weight_grads"):
        sib_gu = mm(v.rows, kept(0, 1), ((1,), (1,))).astype(BF16)
        sib_dn = mm(kept(1, 1), v.grads, ((1,), (0,))).astype(BF16)
        own_gu = mm(v.rows, kept(0, 0), ((1,), (1,))).astype(BF16)
        own_dn = mm(kept(1, 0), v.grads, ((1,), (0,))).astype(BF16)
    sync(sib_gu=sib_gu, sib_dn=sib_dn, own_gu=own_gu, own_dn=own_dn)

    sync(r4=r4)
    sync(r3=r3)
    back_mid = v.dx_flip + v.r4
    back = v.dx_two[count:] + v.r3
    del v.dx_flip, v.r4, v.r3
    sync(back=back, back_mid=back_mid)
    r1 = home(v.back, OUTWARD, "r1")
    r2 = home(v.back_mid, MIDDLE, "r2")
    got_gu = over(v.sib_gu, SWAP, "got_gu", "dp")
    got_dn = over(v.sib_dn, SWAP, "got_dn", "dp")


    sync(got_dn=got_dn, got_gu=got_gu)
    own_n = v.own_dn + v.got_dn
    own_g = v.own_gu[:, :half] + v.got_gu[:, :half]
    own_u = v.own_gu[:, half:] + v.got_gu[:, half:]
    sync(own_g=own_g, own_u=own_u, own_n=own_n)
    two = v.k_two[0]
    dots = (two[:, count:], v.k_cross[0], v.k_flip[0])
    dots = [two[:, :count]] + [small(d, k, "dot") for k, d in enumerate(dots, 1)]
    sync(dots=dots)
    prob_grad = sum(
        jnp.where(ids == (place ^ k), d.reshape(-1, 1), 0.0) for k, d in enumerate(v.dots)
    )
    sync(r1=r1, r2=r2)
    upstream = sum(x.astype(F32) for x in (v.up_own, v.up_near, v.r1, v.r2)).astype(BF16)
    return (
        upstream[None],
        prob_grad[None],
        v.own_g[None, None],
        v.own_u[None, None],
        v.own_n[None, None],
    )


def per_device(tokens, out_grad, expert_ids, route_probs, gate_weight, up_weight, down_weight):
    count, top = expert_ids.shape[1:]
    groups = lax.axis_size("expert")
    whole_blocks = 2 * count * top // groups >= count
    plan = line_plan if groups == 4 and lax.axis_size("dp") == 2 and whole_blocks else exchange_plan
    return plan(tokens, out_grad, expert_ids, route_probs, gate_weight, up_weight, down_weight)


def solution(mesh):
    in_specs = (
        P("section", ("dp", "expert"), None),
        P("section", ("dp", "expert"), None),
        P("section", ("dp", "expert"), None),
        P("section", ("dp", "expert"), None),
        P("section", "expert", None, "dp"),
        P("section", "expert", None, "dp"),
        P("section", "expert", "dp", None),
    )
    out_specs = (
        P("section", ("dp", "expert"), None),
        P("section", ("dp", "expert"), None),
        P("section", "expert", None, "dp"),
        P("section", "expert", None, "dp"),
        P("section", "expert", "dp", None),
    )
    return jax.shard_map(
        per_device, mesh=mesh, in_specs=in_specs, out_specs=out_specs, check_vma=False
    )
```

```python
import functools
import types

import jax
import jax.numpy as jnp
from jax import lax
from jax.experimental import pallas as pl
from jax.experimental.pallas import tpu as pltpu
from jax.sharding import PartitionSpec as P


def from_behind(shard, axis, by):
    length = lax.axis_size(axis)
    return lax.ppermute(shard, axis, [(i, (i + by) % length) for i in range(length)])


def expert_grads(rows_in, grads_in, weights_in, gate_part, up_part, down_part):
    contract_last = (((1,), (1,)), ((), ()))
    contract_first = (((0,), (0,)), ((), ()))
    gate_pre = jnp.dot(rows_in, gate_part, preferred_element_type=jnp.float32)
    up_pre = jnp.dot(rows_in, up_part, preferred_element_type=jnp.float32)
    sigmoid_gate = jax.nn.sigmoid(gate_pre)
    activated = gate_pre * sigmoid_gate * up_pre
    scaled_act = (weights_in[:, None] * activated).astype(jnp.bfloat16)
    hidden_grad = lax.dot_general(
        grads_in, down_part, contract_last, preferred_element_type=jnp.float32
    )
    prob_part = jnp.sum(activated * hidden_grad, axis=1)
    hidden_scaled = weights_in[:, None] * hidden_grad
    gate_grad = (
        hidden_scaled * up_pre * sigmoid_gate * (1.0 + gate_pre * (1.0 - sigmoid_gate))
    ).astype(jnp.bfloat16)
    up_grad = (hidden_scaled * gate_pre * sigmoid_gate).astype(jnp.bfloat16)
    route_dx = lax.dot_general(
        gate_grad, gate_part, contract_last, preferred_element_type=jnp.float32
    ) + lax.dot_general(up_grad, up_part, contract_last, preferred_element_type=jnp.float32)
    grad_gate = lax.dot_general(
        rows_in, gate_grad, contract_first, preferred_element_type=jnp.float32
    )
    grad_up = lax.dot_general(rows_in, up_grad, contract_first, preferred_element_type=jnp.float32)
    grad_down = lax.dot_general(
        scaled_act, grads_in, contract_first, preferred_element_type=jnp.float32
    )
    return (route_dx, prob_part, grad_gate, grad_up, grad_down)


def exchange_plan(tokens, out_grad, expert_ids, route_probs, gate_weight, up_weight, down_weight):
    local_tokens = tokens[0]
    local_grads = out_grad[0]
    tok_count, row_width = local_tokens.shape
    top_count = expert_ids.shape[2]
    groups = lax.axis_size("expert")
    capacity = 2 * tok_count * top_count // groups
    slots_all = groups * capacity
    route_ids = expert_ids[0].reshape(-1)
    hit_table = (route_ids[:, None] == jnp.arange(groups, dtype=jnp.int32)[None, :]).astype(
        jnp.int32
    )
    before = jnp.cumsum(hit_table, axis=0) - hit_table
    slot_rank = jnp.sum(before * hit_table, axis=1)
    slot_of = route_ids * capacity + slot_rank
    placed = slot_of[None, :] == jnp.arange(slots_all, dtype=jnp.int32)[:, None]
    per_token = jnp.any(placed.reshape(slots_all, tok_count, top_count), axis=2).astype(
        jnp.bfloat16
    )
    send_rows = jnp.dot(per_token, local_tokens, preferred_element_type=jnp.float32).astype(
        jnp.bfloat16
    )
    send_grads = jnp.dot(per_token, local_grads, preferred_element_type=jnp.float32).astype(
        jnp.bfloat16
    )
    probs_flat = route_probs[0].reshape(-1)
    send_probs = jnp.sum(jnp.where(placed, probs_flat[None, :], 0.0), axis=1)
    recv_rows, recv_grads, recv_probs = (
        lax.all_to_all(
            send_rows.reshape(groups, capacity, row_width),
            "expert",
            split_axis=0,
            concat_axis=0,
            tiled=True,
        ),
        lax.all_to_all(
            send_grads.reshape(groups, capacity, row_width),
            "expert",
            split_axis=0,
            concat_axis=0,
            tiled=True,
        ),
        lax.all_to_all(
            send_probs.reshape(groups, capacity).astype(jnp.bfloat16),
            "expert",
            split_axis=0,
            concat_axis=0,
            tiled=True,
        ).astype(jnp.float32),
    )
    recv_rows = recv_rows.reshape(slots_all, row_width)
    recv_grads = recv_grads.reshape(slots_all, row_width)
    recv_probs = recv_probs.reshape(slots_all)
    gate_part = gate_weight[0, 0]
    up_part = up_weight[0, 0]
    down_part = down_weight[0, 0]
    gate_full, up_full, down_full = (
        lax.all_gather(gate_part, "dp", axis=1, tiled=True),
        lax.all_gather(up_part, "dp", axis=1, tiled=True),
        lax.all_gather(down_part, "dp", axis=0, tiled=True),
    )
    route_dx, prob_part, grad_gate, grad_up, grad_down = expert_grads(
        recv_rows, recv_grads, recv_probs, gate_full, up_full, down_full
    )
    grad_gate, grad_up, grad_down = (
        lax.psum_scatter(
            grad_gate.astype(jnp.bfloat16), "dp", scatter_dimension=1, tiled=True
        ).astype(jnp.float32),
        lax.psum_scatter(
            grad_up.astype(jnp.bfloat16), "dp", scatter_dimension=1, tiled=True
        ).astype(jnp.float32),
        lax.psum_scatter(
            grad_down.astype(jnp.bfloat16), "dp", scatter_dimension=0, tiled=True
        ).astype(jnp.float32),
    )
    back_rows, back_probs = (
        lax.all_to_all(
            route_dx.astype(jnp.bfloat16).reshape(groups, capacity, row_width),
            "expert",
            split_axis=0,
            concat_axis=0,
            tiled=True,
        ),
        lax.all_to_all(
            prob_part.reshape(groups, capacity).astype(jnp.bfloat16),
            "expert",
            split_axis=0,
            concat_axis=0,
            tiled=True,
        ).astype(jnp.float32),
    )
    token_grad = lax.dot_general(
        per_token,
        back_rows.reshape(slots_all, row_width),
        (((0,), (0,)), ((), ())),
        preferred_element_type=jnp.float32,
    ).astype(jnp.bfloat16)
    route_grad = jnp.sum(jnp.where(placed, back_probs.reshape(slots_all)[:, None], 0.0), axis=0)
    route_grad = route_grad.reshape(tok_count, top_count)
    upstream = from_behind(token_grad, "section", -1)
    return (
        upstream[None],
        route_grad[None],
        grad_gate.astype(jnp.bfloat16)[None, None],
        grad_up.astype(jnp.bfloat16)[None, None],
        grad_down.astype(jnp.bfloat16)[None, None],
    )


INWARD = [(0, 1), (3, 2)]
OUTWARD = [(1, 0), (2, 3)]
MIDDLE = [(1, 2), (2, 1)]
PAIRS = INWARD + OUTWARD
SWAP = [(0, 1), (1, 0)]
F32, BF16 = jnp.float32, jnp.bfloat16


def gather_kernel(places, *refs):
    count = len(places)
    sources, outs, sems = refs[:count], refs[count:-1], refs[-1]
    copies = []
    for i, (source, (out, rows, cols)) in enumerate(zip(sources, places)):
        target = outs[out].at[pl.ds(rows, source.shape[0]), pl.ds(cols, source.shape[1])]
        copies.append(pltpu.make_async_copy(source, target, sems.at[i]))
    for copy in copies:
        copy.start()
    for copy in copies:
        copy.wait()


def gather(name, shapes, *pieces):
    anywhere = pl.BlockSpec(memory_space=pl.ANY)
    return pl.pallas_call(
        functools.partial(gather_kernel, [piece[1:] for piece in pieces]),
        out_shape=[pltpu.VMEM(dims, pieces[0][0].dtype) for dims in shapes],
        in_specs=[anywhere] * len(pieces),
        out_specs=[pl.BlockSpec(memory_space=pltpu.VMEM)] * len(shapes),
        scratch_shapes=[pltpu.SemaphoreType.DMA((len(pieces),))],
        compiler_params=pltpu.CompilerParams(vmem_limit_bytes=16 << 20),
        cost_estimate=pl.CostEstimate(flops=0, bytes_accessed=1 << 20, transcendentals=0),
        name=name,
    )(*(piece[0] for piece in pieces))


def line_plan(tokens, out_grad, expert_ids, route_probs, gate_weight, up_weight, down_weight):
    place = lax.axis_index("expert")
    inner = (place == 1) | (place == 2)
    tok, grd = tokens[0], out_grad[0]
    count, width = tok.shape
    ids, probs = expert_ids[0], route_probs[0]
    half = gate_weight.shape[3]

    def over(x, pairs, name, axis="expert"):
        with jax.named_scope(name):
            return lax.ppermute(x, axis, pairs)

    def mm(a, b, dims):
        return lax.dot_general(a, b, (dims, ((), ())), preferred_element_type=F32)

    def pick(a, b):
        return jnp.where(inner, a, b)

    def small(x, k, name):
        return over(x, [(i, i ^ k) for i in range(4)], name)

    v = types.SimpleNamespace(
        tok=tok, grd=grd, gate=gate_weight[0, 0], up=up_weight[0, 0], own_d=down_weight[0, 0]
    )

    def sync(**ready):
        vars(v).update(ready)
        vars(v).update(lax.optimization_barrier(vars(v)))

    def rows_of(x, c):
        part = x.shape[0] // 2
        return x[c * part : (c + 1) * part]

    def ahead(rows, w):
        with jax.named_scope("ahead"):
            return mm(w, rows, ((0,), (1,)))

    def ahead_both(rows):
        return [ahead(rows, v.own_w), ahead(rows, v.sib_w)]

    def behind(grads, parts, p):
        with jax.named_scope("behind"):
            dots, halves, dx = 0.0, [], 0.0
            both_hidden = mm(v.all_d, grads, ((1,), (1,)))
            for side, (pre, w) in enumerate(zip(parts, (v.own_w, v.sib_w))):
                gate, up = pre[:half], pre[half:]
                sig = jax.nn.sigmoid(gate)
                silu = gate * sig
                act = silu * up
                by_gate = up * sig * (1.0 + gate * (1.0 - sig))
                hidden = both_hidden[side * half :][:half]
                dots = dots + jnp.sum(act * hidden, axis=0, keepdims=True)
                scaled = p * hidden
                both = jnp.concatenate([scaled * by_gate, scaled * silu], axis=0).astype(BF16)
                dx = dx + mm(both, w, ((0,), (1,)))
                halves.append((both, (p * act).astype(BF16)))
            return dx.astype(BF16), (dots, halves)

    columns = [
        jnp.sum(jnp.where(ids == (place ^ k), probs, 0.0), axis=1).reshape(1, -1) for k in range(4)
    ]
    v.columns = columns
    t_near = over(v.tok, PAIRS, "t_near")
    t_mid_in = over(v.tok, MIDDLE, "t_mid_in")
    p_near, p_cross, p_flip = (small(v.columns[k], k, "p") for k in (1, 2, 3))
    (own_w,) = gather("own_w", [(width, 2 * half)], (v.gate, 0, 0, 0), (v.up, 0, 0, half))
    sync(own_w=own_w)

    sync(t_near=t_near, t_mid_in=t_mid_in, p_near=p_near, p_cross=p_cross, p_flip=p_flip)
    g_near = over(v.grd, PAIRS, "g_near")
    t_mid_out = over(v.t_mid_in, OUTWARD, "t_mid_out")
    t_far_in = over(v.t_near, MIDDLE, "t_far_in")
    sib_w = over(v.own_w, SWAP, "sib_w", "dp")
    sib_d = over(v.own_d, SWAP, "sib_d", "dp")
    t_two = jnp.concatenate([v.tok, v.t_near], axis=0)
    a_two = ahead(t_two, v.own_w)
    sync(t_two=t_two, a_two=a_two)

    sync(g_near=g_near)
    g_far_in = over(v.g_near, MIDDLE, "g_far_in")
    sync(t_far_in=t_far_in, sib_w=sib_w, sib_d=sib_d)
    t_far_out = over(v.t_far_in, OUTWARD, "t_far_out")
    sib_w, all_d = gather(
        "sib_w",
        [(width, 2 * half), (2 * half, width)],
        (v.sib_w, 0, 0, 0),
        (v.own_d, 1, 0, 0),
        (v.sib_d, 1, half, 0),
    )
    del v.gate, v.up, v.own_d, v.sib_d
    a_two = [v.a_two, ahead(v.t_two, sib_w)]
    del v.t_two
    sync(a_two=a_two, sib_w=sib_w, all_d=all_d)

    two = jnp.concatenate([v.grd, v.g_near], axis=0)
    dx_two, k_two = behind(two, v.a_two, jnp.concatenate([v.columns[0], v.p_near], axis=1))
    del v.p_near, v.a_two, v.columns
    sync(dx_two=dx_two, k_two=k_two)
    n = lax.axis_size("section")

    def home(x, pairs, name):
        steps = [(4 * i + a, (i - 1) % n * 4 + b) for i in range(n) for a, b in pairs]
        return over(x, steps, name, ("section", "expert"))

    up_own = over(v.dx_two[:count], [(i, (i - 1) % n) for i in range(n)], "up", "section")
    up_near = home(v.dx_two[count:], INWARD, "up")
    d_near = small(v.k_two[0][:, count:], 1, "dot")

    sync(t_mid_out=t_mid_out, g_far_in=g_far_in)
    g_far_out = over(v.g_far_in, OUTWARD, "g_far_out")
    g_mid_in = over(v.grd, MIDDLE, "g_mid_in")

    sync(t_far_out=t_far_out)
    t_cross, t_flip = pick(v.t_far_in, v.t_mid_out), pick(v.t_mid_in, v.t_far_out)
    del v.t_far_in, v.t_mid_out, v.t_mid_in, v.t_far_out
    a_far = ahead_both(jnp.concatenate([t_cross, t_flip], axis=0))
    sync(t_cross=t_cross, t_flip=t_flip, a_far=a_far)

    sync(g_mid_in=g_mid_in)
    g_mid_out = over(v.g_mid_in, OUTWARD, "g_mid_out")
    rows = jnp.concatenate([v.tok.T, v.t_near.T, v.t_cross.T, v.t_flip.T], axis=1)
    del v.tok, v.t_near, v.t_cross, v.t_flip
    sync(rows=rows)
    sync(g_far_out=g_far_out)
    g_flip = pick(v.g_mid_in, v.g_far_out)
    dx_flip, k_flip = behind(g_flip, [a[:, count:] for a in v.a_far], v.p_flip)
    del v.g_mid_in, v.g_far_out, v.p_flip
    sync(g_flip=g_flip, dx_flip=dx_flip, k_flip=k_flip)
    r5 = over(v.dx_flip, INWARD, "r5")

    sync(g_mid_out=g_mid_out)
    g_cross = pick(v.g_far_in, v.g_mid_out)
    dx_cross, k_cross = behind(g_cross, [a[:, :count] for a in v.a_far], v.p_cross)
    del v.g_far_in, v.g_mid_out, v.a_far, v.p_cross
    sync(g_cross=g_cross, dx_cross=dx_cross, k_cross=k_cross)
    r4 = over(v.dx_cross, INWARD, "r4")

    sync(r5=r5, up_own=up_own, up_near=up_near, d_near=d_near)
    back = v.dx_cross + v.r5
    del v.dx_cross, v.r5
    sync(back=back)
    r3 = over(v.back, MIDDLE, "r3")
    grads = jnp.concatenate([v.grd, v.g_near, v.g_cross, v.g_flip], axis=0)
    del v.grd, v.g_near, v.g_cross, v.g_flip
    sync(grads=grads)
    del v.own_w, v.sib_w, v.all_d, v.back

    def kept(which, side, first=0, last=None):
        slots = [k[1][side][which][first:last] for k in (v.k_two, v.k_cross, v.k_flip)]
        return jnp.concatenate(slots, axis=1)

    with jax.named_scope("weight_grads"):
        sib_gu = mm(v.rows, kept(0, 1), ((1,), (1,))).astype(BF16)
        sib_dn = mm(kept(1, 1), v.grads, ((1,), (0,))).astype(BF16)
        own_gu = mm(v.rows, kept(0, 0), ((1,), (1,))).astype(BF16)
        own_dn = mm(kept(1, 0), v.grads, ((1,), (0,))).astype(BF16)
    sync(sib_gu=sib_gu, sib_dn=sib_dn, own_gu=own_gu, own_dn=own_dn)

    sync(r4=r4)
    sync(r3=r3)
    back_mid = v.dx_flip + v.r4
    back = v.dx_two[count:] + v.r3
    del v.dx_flip, v.r4, v.r3
    sync(back=back, back_mid=back_mid)
    r1 = home(v.back, OUTWARD, "r1")
    r2 = home(v.back_mid, MIDDLE, "r2")
    got_gu = over(v.sib_gu, SWAP, "got_gu", "dp")
    got_dn = over(v.sib_dn, SWAP, "got_dn", "dp")


    sync(got_dn=got_dn, got_gu=got_gu)
    own_n = v.own_dn + v.got_dn
    own_g = v.own_gu[:, :half] + v.got_gu[:, :half]
    own_u = v.own_gu[:, half:] + v.got_gu[:, half:]
    sync(own_g=own_g, own_u=own_u, own_n=own_n)
    dots = [small(v.k_cross[0], 2, "dot"), small(v.k_flip[0], 3, "dot")]
    sync(r1=r1, r2=r2)
    upstream = sum(x.astype(F32) for x in (v.up_own, v.up_near, v.r1, v.r2)).astype(BF16)
    dots = [v.k_two[0][:, :count], v.d_near] + dots
    prob_grad = sum(
        jnp.where(ids == (place ^ k), d.reshape(-1, 1), 0.0) for k, d in enumerate(dots)
    )
    return (
        upstream[None],
        prob_grad[None],
        v.own_g[None, None],
        v.own_u[None, None],
        v.own_n[None, None],
    )


def per_device(tokens, out_grad, expert_ids, route_probs, gate_weight, up_weight, down_weight):
    count, top = expert_ids.shape[1:]
    groups = lax.axis_size("expert")
    whole_blocks = 2 * count * top // groups >= count
    plan = line_plan if groups == 4 and lax.axis_size("dp") == 2 and whole_blocks else exchange_plan
    return plan(tokens, out_grad, expert_ids, route_probs, gate_weight, up_weight, down_weight)


def solution(mesh):
    in_specs = (
        P("section", ("dp", "expert"), None),
        P("section", ("dp", "expert"), None),
        P("section", ("dp", "expert"), None),
        P("section", ("dp", "expert"), None),
        P("section", "expert", None, "dp"),
        P("section", "expert", None, "dp"),
        P("section", "expert", "dp", None),
    )
    out_specs = (
        P("section", ("dp", "expert"), None),
        P("section", ("dp", "expert"), None),
        P("section", "expert", None, "dp"),
        P("section", "expert", None, "dp"),
        P("section", "expert", "dp", None),
    )
    return jax.shard_map(
        per_device, mesh=mesh, in_specs=in_specs, out_specs=out_specs, check_vma=False
    )
```
